512 devices in a mesh: gx: 32 (over z, y_lo), gy: 16 (over x, y_hi, core).
Axes of the slice: x: 4, y: 8 (y_hi: 2, y_lo: 4; y = y_hi * 4 + y_lo), z: 8, core: 2. Of those that a mesh axis runs over, the one named last changes fastest.
Arguments:
- fields: bfloat16 [8, 128, 128, 256], P(None, 'gx', 'gy'), may hold values from -6 to 6
- cotangent: bfloat16 [8, 128, 128, 256], P(None, 'gx', 'gy'), may hold values from -6 to 6
- w_down: bfloat16 [3, 3, 3, 32, 8], replicated, may hold values from -0.4375 to 0.4375
- w_mid: bfloat16 [3, 3, 3, 32, 32], replicated, may hold values from -0.21875 to 0.21875
- w_up: bfloat16 [3, 3, 3, 8, 32], replicated, may hold values from -0.5 to 0.5
Outputs:
- mapped: bfloat16 [8, 128, 128, 256], P(None, 'gx', 'gy')
- grad_fields: bfloat16 [8, 128, 128, 256], P(None, 'gx', 'gy')
- grad_w_down: float32 [3, 3, 3, 32, 8], replicated
- grad_w_mid: float32 [3, 3, 3, 32, 32], replicated
- grad_w_up: float32 [3, 3, 3, 8, 32], replicated
The draws below stay inside these ranges and needn't reach their ends.
All inputs are finite; a program needn't handle non-finite values.
Results may differ from the reference program's by a relative error of at most 0.0052.
Values may be sent and summed in bfloat16 or wider, within the bound.
No kernel may reach another device: no remote copies, remote signals or barrier semaphores. Data moves between devices by JAX's collectives and lax.ppermute only.
A program may use at most 128 MiB of HBM per device.

```python
import jax
import jax.numpy as jnp
from jax import lax

CHAN = 8
HID = 32
NZ = 256
NX = 128
NY = 128


def block_levels(own_key, dims, cuts, smallest, largest):
    def one(position, blocks):
        steps = jax.random.uniform(jax.random.fold_in(jax.random.fold_in(own_key, 6), position), (blocks,), jnp.float32, smallest / len(cuts), largest / len(cuts))
        return jnp.repeat(jnp.exp(steps), dims[position] // blocks).reshape((-1,) + (1,) * (len(dims) - position - 1))

    loudness = one(*cuts[0])
    for cut in cuts[1:]:
        loudness = loudness * one(*cut)
    return loudness


def scatter_about(rng, dims, spread, reach, split=(), dtype=jnp.bfloat16):
    loudness = block_levels(rng, dims, split, -0.22, 0.18) if split else 1.0
    values = jax.random.normal(rng, dims, jnp.float32) * spread * loudness
    return jnp.minimum(jnp.maximum(values, -reach), reach).astype(dtype)


def setup_inputs(seed: int = 0) -> dict:
    key_list = jax.random.split(jax.random.key(seed), 6)
    fields = scatter_about(key_list[0], (CHAN, NX, NY, NZ), 1.0, 6.0, ((1, 32), (2, 16)))
    cotangent = scatter_about(key_list[1], (CHAN, NX, NY, NZ), 1.0, 6.0, ((1, 32), (2, 16)))
    w_down = scatter_about(key_list[2], (3, 3, 3, HID, CHAN), (27 * CHAN) ** -0.5, 0.4375)
    w_mid = scatter_about(key_list[3], (3, 3, 3, HID, HID), (27 * HID) ** -0.5, 0.21875)
    w_up = scatter_about(key_list[4], (3, 3, 3, CHAN, HID), (4 * HID) ** -0.5, 0.5)
    return {"fields": fields, "cotangent": cotangent, "w_down": w_down, "w_mid": w_mid, "w_up": w_up}


numbers = ('NCDHW', 'OIDHW', 'NCDHW')

def act(v):
    return 0.2 * v + 0.8 * v * jax.nn.sigmoid(v)

def slope(v):
    s = jax.nn.sigmoid(v)
    return 0.2 + 0.8 * (s + v * s * (1.0 - s))

def down_op(x, w):
    padded = jnp.pad(x, ((0, 0), (1, 0), (1, 0), (1, 0)), mode='wrap')
    kernel = jnp.transpose(w, (3, 4, 0, 1, 2))
    return lax.conv_general_dilated(padded[None], kernel, (2, 2, 2), 'VALID', dimension_numbers=numbers, precision=lax.Precision.HIGHEST)[0]

def same_op(x, w):
    padded = jnp.pad(x, ((0, 0), (1, 1), (1, 1), (1, 1)), mode='wrap')
    kernel = jnp.transpose(w, (3, 4, 0, 1, 2))
    return lax.conv_general_dilated(padded[None], kernel, (1, 1, 1), 'VALID', dimension_numbers=numbers, precision=lax.Precision.HIGHEST)[0]

def up_op(h, w):
    shape = (w.shape[3], 2 * h.shape[1], 2 * h.shape[2], 2 * h.shape[3])
    swapped = jnp.swapaxes(w, 3, 4)
    _, pull = jax.vjp(lambda x: down_op(x, swapped), jnp.zeros(shape, jnp.float32))
    return pull(h)[0]

def reference(fields, cotangent, w_down, w_mid, w_up):
    f32 = jnp.float32
    field_f = fields.astype(f32)
    cot_f = cotangent.astype(f32)
    wd = w_down.astype(f32)
    wm = w_mid.astype(f32)
    wu = w_up.astype(f32)
    h1_pre = down_op(field_f, wd)
    h1 = act(h1_pre).astype(jnp.bfloat16).astype(f32)
    h2_pre = same_op(h1, wm)
    h2 = act(h2_pre).astype(jnp.bfloat16).astype(f32)
    mapped = (field_f + up_op(h2, wu)).astype(jnp.bfloat16)
    wu_swapped = jnp.swapaxes(wu, 3, 4)
    dh2 = down_op(cot_f, wu_swapped)
    dh2_pre = (dh2 * slope(h2_pre)).astype(jnp.bfloat16).astype(f32)
    _, pull_mid = jax.vjp(lambda x: same_op(x, wm), h1)
    dh1 = pull_mid(dh2_pre)[0]
    dh1_pre = (dh1 * slope(h1_pre)).astype(jnp.bfloat16).astype(f32)
    grad_fields = (cot_f + up_op(dh1_pre, jnp.swapaxes(wd, 3, 4))).astype(jnp.bfloat16)
    _, pull_wd = jax.vjp(lambda w: down_op(field_f, w), wd)
    grad_w_down = pull_wd(dh1_pre)[0]
    _, pull_wm = jax.vjp(lambda w: same_op(h1, w), wm)
    grad_w_mid = pull_wm(dh2_pre)[0]
    _, pull_wu = jax.vjp(lambda w: down_op(cot_f, w), wu_swapped)
    grad_w_up = jnp.swapaxes(pull_wu(h2)[0], 3, 4)
    return (mapped, grad_fields, grad_w_down, grad_w_mid, grad_w_up)
```

```python
import jax
import jax.numpy as jnp
from jax import lax
from jax.experimental import pallas as pl
from jax.experimental.pallas import tpu as pltpu
from jax.sharding import PartitionSpec as P

BF = jnp.bfloat16
F32 = jnp.float32
LANES = 128
LOCAL = [(i, j) for i in range(2) for j in range(4)]
UPPER = LOCAL + [(0, 4), (1, 4)] + [(2, j) for j in range(5)]
ROWS = 384


def shift(x, axis, by):
    devices = lax.axis_size(axis)
    return lax.ppermute(x, axis, [(i, (i + by) % devices) for i in range(devices)])


def call(body, outs, args, scratch=(), flops=10**8):
    moved = 2 * 10**6
    return pl.pallas_call(
        body,
        out_shape=[jax.ShapeDtypeStruct(s, d) for s, d in outs],
        in_specs=[pl.BlockSpec(memory_space=pltpu.VMEM)] * len(args),
        out_specs=[pl.BlockSpec(memory_space=pltpu.VMEM)] * len(outs),
        scratch_shapes=[pltpu.VMEM(s, d) for s, d in scratch],
        compiler_params=pltpu.CompilerParams(vmem_limit_bytes=32 * 2**20),
        cost_estimate=pl.CostEstimate(flops=flops, bytes_accessed=moved, transcendentals=0),
    )(*args)


def dot(a, b):
    return lax.dot_general(a, b, (((1,), (0,)), ((), ())), preferred_element_type=F32)


def dot_nt(a, b):
    return lax.dot_general(a, b, (((1,), (1,)), ((), ())), preferred_element_type=F32)


def split_z():
    z = lax.broadcasted_iota(jnp.int32, (256, 256), 0)
    k = lax.broadcasted_iota(jnp.int32, (256, 256), 1)
    return (z == 2 * (k & 127) + (k >> 7)).astype(F32).astype(BF)


def join_z():
    k = lax.broadcasted_iota(jnp.int32, (256, 256), 0)
    z = lax.broadcasted_iota(jnp.int32, (256, 256), 1)
    return (z == 2 * (k & 127) + (k >> 7)).astype(F32).astype(BF)


def slab_order(dim):
    r = lax.broadcasted_iota(jnp.int32, (512, 512), dim)
    s = lax.broadcasted_iota(jnp.int32, (512, 512), 1 - dim)
    source = ((r >> 3) & 1) * 256 + (r & 7) * 32 + (r >> 7) * 8 + ((r >> 4) & 7)
    return (s == source).astype(F32).astype(BF)


def to_slabs_kernel(f_ref, g_ref, f_out, g_out, up_out, down_out):
    halves = split_z()
    order = slab_order(0)
    for ref, out in ((f_ref, f_out), (g_ref, g_out)):
        z = dot(ref[...], halves).astype(BF)
        z = jnp.concatenate([z[:, :LANES], z[:, LANES:]], 0)
        out[...] = dot(order, z).astype(BF).reshape(4, 8, 16, LANES)
    up_out[:, 0:3] = f_out[:, 5:8]
    up_out[:, 3:4] = g_out[:, 7:8]
    down_out[...] = f_out[:, 0:2]


def rolled_odd(slab):
    return pltpu.roll(slab.astype(F32)[8:], 1, 1)


def act_and_slope(v):
    s = jax.nn.sigmoid(v)
    return 0.2 * v + 0.8 * v * s, 0.2 + 0.8 * (s + v * s * (1.0 - s))


def three(v):
    return jnp.concatenate([pltpu.roll(v, 1, 1), v, pltpu.roll(v, LANES - 1, 1)], 0).astype(BF)


def fill_columns(out, n, slab, pair, i, j):
    for a in range(3):
        x = 2 * i + a - 1
        tiles = [slab(x, 2 * j - 1), slab(x, 2 * j), slab(x, 2 * j + 1), pair(x, j - 1), pair(x, j)]
        for t, tile in enumerate(tiles):
            row = 80 * a + 16 * t
            out[row : row + 16, n * LANES : (n + 1) * LANES] = tile


def grad_block(cols, h, rows, step):
    n = h.shape[1]
    total = None
    for k in range(4):
        size = min(step, rows - step * k)
        padded = jnp.concatenate(
            [jnp.zeros((32 * k, n), BF)] * (k > 0) + [h] + [jnp.zeros((96 - 32 * k, n), BF)] * (k < 3), 0
        )
        term = dot_nt(cols[step * k : step * k + size, :n], padded)
        if size < step:
            term = jnp.concatenate([term, jnp.zeros((step - size, LANES), F32)], 0)
        total = term if total is None else total + term
    return total


def forward_kernel(
    f_ref, g_ref, ylo, yhi, xlo, xhi, wd, wm, wg,
    slope_out, h1_out, h2_out, d2_out, fcol_out, gup_out, up_out, down_out,
    fpair, gpair, h1_three, xcol, mcol, gcol,
):
    def f(x, y):
        if x < 0:
            return xlo[(x + 3) * 13 + y + 3]
        if x > 3:
            return xhi[(x - 4) * 13 + y + 3]
        return ylo[x, y + 3] if y < 0 else yhi[x, y - 8] if y > 7 else f_ref[x, y]

    def g(x, y):
        if x < 0:
            return xlo[39 + y + 1]
        return ylo[x, 3] if y < 0 else g_ref[x, y]

    zero = jnp.zeros((8, LANES), F32)
    for x in range(-3, 6):
        for j in range(-2, 5):
            first = zero if j == -2 else rolled_odd(f(x, 2 * j))
            fpair[x + 3, j + 2] = jnp.concatenate([first, rolled_odd(f(x, 2 * j + 1))], 0).astype(BF)
    for x in range(-1, 4):
        for j in range(-1, 4):
            first = zero if j == -1 else rolled_odd(g(x, 2 * j))
            gpair[x + 1, j + 1] = jnp.concatenate([first, rolled_odd(g(x, 2 * j + 1))], 0).astype(BF)

    def f_pair(x, j):
        return fpair[x + 3, j + 2]

    def g_pair(x, j):
        return gpair[x + 1, j + 1]

    for n, (i, j) in enumerate(LOCAL):
        fill_columns(fcol_out, n, f, f_pair, i, j)
        fill_columns(gcol, n, g, g_pair, i, j)
    rest = [(i, j) for i in range(-1, 3) for j in range(-1, 5) if (i, j) not in LOCAL]
    for n, (i, j) in enumerate(rest):
        fill_columns(xcol, n, f, f_pair, i, j)

    def put_h1(cells, columns):
        wide = len(cells) * LANES
        v, s = act_and_slope(dot(wd[...], columns))
        for n, (i, j) in enumerate(cells):
            lanes = slice(n * LANES, (n + 1) * LANES)
            h1_three[i + 1, j + 1] = three(v[:, lanes])
            if i >= 0 and j >= 0:
                slope_out[i * 5 + j] = s[:, lanes]
            if (i, j) in LOCAL:
                h1_out[:, LOCAL.index((i, j)) * LANES : (LOCAL.index((i, j)) + 1) * LANES] = v[:, lanes].astype(BF)

    for start in range(0, 8, 4):
        put_h1(LOCAL[start : start + 4], fcol_out[:, start * LANES : (start + 4) * LANES])
    for start in range(0, 16, 4):
        put_h1(rest[start : start + 4], xcol[:, start * LANES : (start + 4) * LANES])

    for n, (i, j) in enumerate(LOCAL):
        for a in range(3):
            for b in range(3):
                row = 96 * (3 * a + b)
                mcol[row : row + 96, n * LANES : (n + 1) * LANES] = h1_three[i + a, j + b]

    for start in range(0, 8, 4):
        lanes = slice(start * LANES, (start + 4) * LANES)
        v, s = act_and_slope(dot(wm[...], mcol[:, lanes]))
        h2_out[:, lanes] = v.astype(BF)
        d2_out[:, lanes] = (dot(wg[...], gcol[:, lanes]) * s).astype(BF)

    gup_out[...] = grad_block(gcol, h2_out[...], 240, 64)
    for i in range(2):
        at = 4 * i * LANES
        up_out[i] = d2_out[:, at + 3 * LANES : at + 4 * LANES]
        down_out[i] = d2_out[:, at : at + LANES]
        down_out[2 + i] = d2_out[:, at + LANES : at + 2 * LANES]
        down_out[4 + i] = h2_out[:, at : at + LANES]


def backward_kernel(
    d2, ylo, yhi, xlo, xhi, slope, h1, fcol, gup, wb, grads_out, d1_out, d2_three, mcol,
):
    def d(i, j):
        if i < 0:
            return xlo[j + 1]
        if i > 1:
            return xhi[(i - 2) * 7 + j + 1]
        if j < 0:
            return ylo[i]
        if j > 3:
            return yhi[2 * (j - 4) + i]
        at = (4 * i + j) * LANES
        return d2[:, at : at + LANES]

    for i in range(-1, 4):
        for j in range(-1, 6):
            d2_three[i + 1, j + 1] = three(d(i, j).astype(F32))
    for n, (i, j) in enumerate(UPPER):
        for a in range(3):
            for b in range(3):
                row = 96 * (3 * a + b)
                mcol[row : row + 96, n * LANES : (n + 1) * LANES] = d2_three[i + a, j + b]
    for start in range(0, 15, 4):
        cells = UPPER[start : start + 4]
        v = dot(wb[...], mcol[:, start * LANES : (start + len(cells)) * LANES])
        for n, (i, j) in enumerate(cells):
            at = (start + n) * LANES
            d1_out[:, at : at + LANES] = (v[:, n * LANES : (n + 1) * LANES] * slope[i * 5 + j]).astype(BF)
    grads_out[0:224] = grad_block(mcol, h1[...], 864, 224)
    grads_out[224:288] = grad_block(fcol, d1_out[:, : 8 * LANES], 240, 64)
    grads_out[288:352] = gup[...]
    grads_out[352:ROWS] = jnp.zeros((ROWS - 352, LANES), F32)


def outputs_kernel(f_ref, g_ref, h2, yhi, xhi, d1, wu, wv, mapped_out, grad_out, ucol, slabs):
    def h(i, j):
        if i > 1:
            return xhi[14 + j]
        if j > 3:
            return yhi[4 + i]
        at = (4 * i + j) * LANES
        return h2[:, at : at + LANES]

    def p(i, j):
        at = UPPER.index((i, j)) * LANES
        return d1[:, at : at + LANES]

    joined = join_z()
    order = slab_order(1)
    for cell, w, base, out in ((h, wu, f_ref, mapped_out), (p, wv, g_ref, grad_out)):
        two = {}
        for i, j in UPPER:
            v = cell(i, j).astype(F32)
            two[i, j] = jnp.concatenate([v, pltpu.roll(v, LANES - 1, 1)], 0).astype(BF)
        for n, (i, j) in enumerate(LOCAL):
            for k in range(4):
                ucol[64 * k : 64 * k + 64, n * LANES : (n + 1) * LANES] = two[i + k // 2, j + k % 2]
        for start in range(0, 8, 2):
            up = dot(w[...], ucol[:, start * LANES : (start + 2) * LANES])
            for n in range(2):
                i, j = LOCAL[start + n]
                for k in range(4):
                    x, y = 2 * i + k // 2, 2 * j + k % 2
                    row = 16 * (8 * x + y)
                    added = base[x, y].astype(F32) + up[16 * k : 16 * k + 16, n * LANES : (n + 1) * LANES]
                    slabs[row : row + 16] = added.astype(BF)
        z = dot(order, slabs[...]).astype(BF)
        out[...] = dot(jnp.concatenate([z[:256], z[256:]], 1), joined).astype(BF)


def tap_rows(rows):
    order = [(0, 1), (0, 2), (1, 1), (1, 2), (2, 1), (2, 2), None, (0, 0), (1, 0), (2, 0)]
    for a in range(3):
        for m, tap in enumerate(order):
            if tap is not None:
                yield 10 * a + m, 9 * a + 3 * tap[0] + tap[1]


def unpack_kernel(total, down_out, mid_out, up_out):
    for k in range(4):
        part = total[0:224]
        part = pltpu.roll(part, LANES - 32 * k, 1) if k else part
        for s in range(min(7, 27 - 7 * k)):
            mid_out[26 - (7 * k + s)] = part[32 * s : 32 * s + 32, :32]
    flipped = total[224:288].T
    for block, tap in tap_rows(240):
        k, m = block // 8, block % 8
        rows = flipped[32 * k : 32 * k + 32]
        rows = jnp.concatenate([rows, jnp.zeros((32, 64), F32)], 1)
        rows = pltpu.roll(rows, LANES - 8 * m, 1) if m else rows
        down_out[tap] = rows[:, :8]
    for k in range(4):
        part = total[288:352]
        part = pltpu.roll(part, LANES - 32 * k, 1) if k else part
        for block, tap in tap_rows(240):
            if block // 8 == k:
                m = block % 8
                up_out[tap] = part[8 * m : 8 * m + 8, :32]


def down_weights(w):
    none = jnp.zeros_like(w[:, 0, 0])
    blocks = [w[:, 0, 1], w[:, 0, 2], w[:, 1, 1], w[:, 1, 2], w[:, 2, 1], w[:, 2, 2], none, w[:, 0, 0], w[:, 1, 0], w[:, 2, 0]]
    return jnp.transpose(jnp.stack(blocks, 1), (2, 0, 1, 3)).reshape(32, 240)


def up_weights(w):
    none = jnp.zeros_like(w[0, 0, 0])
    pick = ((1, None), (2, 0))
    rows = []
    for p in range(2):
        for q in range(2):
            for r in range(2):
                row = []
                for k in range(8):
                    a, b, d = pick[p][k // 4], pick[q][k // 2 % 2], pick[r][k % 2]
                    row.append(none if None in (a, b, d) else w[a, b, d])
                rows.append(jnp.concatenate(row, 1))
    return jnp.concatenate(rows, 0)


def all_sum(x):
    gx, gy = lax.axis_size("gx"), lax.axis_size("gy")
    part = x.reshape(gx, ROWS // gx, LANES)
    part = lax.all_to_all(part, "gx", 0, 0, tiled=True).sum(0)
    part = jnp.broadcast_to(part[None], (gy,) + part.shape)
    part = lax.all_to_all(part, "gy", 0, 0, tiled=True).sum(0)
    part = jnp.broadcast_to(part[None], (gx,) + part.shape)
    return lax.all_to_all(part, "gx", 0, 0, tiled=True).reshape(ROWS, LANES)


def local(fields, cotangent, w_down, w_mid, w_up):
    wd = down_weights(w_down)
    wg = down_weights(jnp.swapaxes(w_up, 3, 4))
    wm = jnp.transpose(w_mid, (3, 0, 1, 2, 4)).reshape(32, 864)
    wb = jnp.transpose(w_mid[::-1, ::-1, ::-1], (4, 0, 1, 2, 3)).reshape(32, 864)
    wu = up_weights(w_up)
    wv = up_weights(jnp.swapaxes(w_down, 3, 4))

    f, g, up, down = call(
        to_slabs_kernel,
        [((4, 8, 16, LANES), BF)] * 2 + [((4, 4, 16, LANES), BF), ((4, 2, 16, LANES), BF)],
        [fields.reshape(256, 256), cotangent.reshape(256, 256)],
    )
    ylo, yhi = shift(up, "gy", 1), shift(down, "gy", -1)
    f_ext = jnp.concatenate([ylo[:, :3], f, yhi], 1)
    last = jnp.concatenate([f_ext[1:].reshape(39, 16, LANES), ylo[3, 3:4], g[3]], 0)
    xlo = shift(last, "gx", 1)
    xhi = shift(f_ext[:2].reshape(26, 16, LANES), "gx", -1)

    slope, h1, h2, d2, fcol, gup, up, down = call(
        forward_kernel,
        [((15, 32, LANES), F32), ((32, 8 * LANES), BF), ((32, 8 * LANES), BF), ((32, 8 * LANES), BF),
         ((240, 8 * LANES), BF), ((64, LANES), F32), ((2, 32, LANES), BF), ((6, 32, LANES), BF)],
        [f, g, ylo, yhi, xlo, xhi, wd, wm, wg],
        [((9, 7, 16, LANES), BF), ((5, 5, 16, LANES), BF), ((4, 6, 96, LANES), BF),
         ((240, 16 * LANES), BF), ((864, 8 * LANES), BF), ((240, 8 * LANES), BF)],
    )
    ylo, yhi = shift(up, "gy", 1), shift(down, "gy", -1)
    cells = jnp.transpose(d2.reshape(32, 8, LANES), (1, 0, 2))
    last = jnp.concatenate([ylo[1:2], cells[4:8], yhi[1:2], yhi[3:4]], 0)
    first = jnp.concatenate(
        [ylo[0:1], cells[0:4], yhi[0:1], yhi[2:3], last]
        + [h2[None, :, j * LANES : (j + 1) * LANES] for j in range(4)] + [yhi[4:5]], 0
    )
    xlo = shift(last, "gx", 1)
    xhi = shift(first, "gx", -1)

    grads, d1 = call(
        backward_kernel,
        [((ROWS, LANES), F32), ((32, 15 * LANES), BF)],
        [d2, ylo, yhi, xlo, xhi, slope, h1, fcol, gup, wb],
        [((5, 7, 96, LANES), BF), ((864, 15 * LANES), BF)],
    )
    mapped, grad_fields = call(
        outputs_kernel,
        [((256, 256), BF)] * 2,
        [f, g, h2, yhi, xhi, d1, wu, wv],
        [((256, 8 * LANES), BF), ((512, LANES), BF)],
    )
    grad_down, grad_mid, grad_up = call(
        unpack_kernel,
        [((27, 32, 8), F32), ((27, 32, 32), F32), ((27, 8, 32), F32)],
        [all_sum(grads)],
    )
    return (
        mapped.reshape(fields.shape),
        grad_fields.reshape(fields.shape),
        grad_down.reshape(w_down.shape),
        grad_mid.reshape(w_mid.shape),
        grad_up.reshape(w_up.shape),
    )


def solution(mesh):
    in_specs = (P(None, "gx", "gy", None), P(None, "gx", "gy", None), P(), P(), P())
    out_specs = (P(None, "gx", "gy", None), P(None, "gx", "gy", None), P(), P(), P())
    return jax.shard_map(local, mesh=mesh, in_specs=in_specs, out_specs=out_specs, check_vma=False)
```

```python
import jax
import jax.numpy as jnp
from jax import lax
from jax.experimental import pallas as pl
from jax.experimental.pallas import tpu as pltpu
from jax.sharding import Mesh
from jax.sharding import PartitionSpec as P

BF = jnp.bfloat16
F32 = jnp.float32
LANES = 128
LOCAL = [(i, j) for i in range(2) for j in range(4)]
UPPER = LOCAL + [(0, 4), (1, 4)] + [(2, j) for j in range(5)]
AROUND = [(i, j) for i in range(-1, 3) for j in range(-1, 5)]
ROW = 6 * LANES
ROWS = 384
GX = ("z", "yl")
GY = ("x", "yh", "core")


def shift(x, axis, by):
    devices = lax.axis_size(axis)
    return lax.ppermute(x, axis, [(i, (i + by) % devices) for i in range(devices)])


def call(body, outs, args, scratch=(), flops=10**8, space=pltpu.VMEM):
    moved = 2 * 10**6
    return pl.pallas_call(
        body,
        out_shape=[jax.ShapeDtypeStruct(s, d) for s, d in outs],
        in_specs=[pl.BlockSpec(memory_space=space)] * len(args),
        out_specs=[pl.BlockSpec(memory_space=pltpu.VMEM)] * len(outs),
        scratch_shapes=[pltpu.VMEM(*s) if isinstance(s, tuple) else s for s in scratch],
        compiler_params=pltpu.CompilerParams(vmem_limit_bytes=32 * 2**20),
        cost_estimate=pl.CostEstimate(flops=flops, bytes_accessed=moved, transcendentals=0),
    )(*args)


def dot(a, b):
    return lax.dot_general(a, b, (((1,), (0,)), ((), ())), preferred_element_type=F32)


def dot_nt(a, b):
    return lax.dot_general(a, b, (((1,), (1,)), ((), ())), preferred_element_type=F32)


def split_z():
    z = lax.broadcasted_iota(jnp.int32, (256, 256), 0)
    k = lax.broadcasted_iota(jnp.int32, (256, 256), 1)
    return (z == 2 * (k & 127) + (k >> 7)).astype(F32).astype(BF)


def join_z():
    k = lax.broadcasted_iota(jnp.int32, (256, 256), 0)
    z = lax.broadcasted_iota(jnp.int32, (256, 256), 1)
    return (z == 2 * (k & 127) + (k >> 7)).astype(F32).astype(BF)


def slab_order(dim):
    r = lax.broadcasted_iota(jnp.int32, (512, 512), dim)
    s = lax.broadcasted_iota(jnp.int32, (512, 512), 1 - dim)
    source = ((r >> 3) & 1) * 256 + (r & 7) * 32 + (r >> 7) * 8 + ((r >> 4) & 7)
    return (s == source).astype(F32).astype(BF)


def to_slabs_kernel(f_any, g_any, f_out, g_out, up_out, down_out, raw, sems):
    copies = [pltpu.make_async_copy(ref, raw.at[k], sems.at[k]) for k, ref in enumerate((f_any, g_any))]
    for copy in copies:
        copy.start()
    halves = split_z()
    order = slab_order(0)
    for k, out in enumerate((f_out, g_out)):
        copies[k].wait()
        z = dot(raw[k], halves).astype(BF)
        z = jnp.concatenate([z[:, :LANES], z[:, LANES:]], 0)
        out[...] = dot(order, z).astype(BF).reshape(4, 8, 16, LANES)
    up_out[:, 0:3] = f_out[:, 5:8]
    up_out[:, 3:4] = g_out[:, 7:8]
    down_out[...] = f_out[:, 0:2]


def rolled_odd(slab):
    return pltpu.roll(slab.astype(F32)[8:], 1, 1)


def act_and_slope(v):
    s = jax.nn.sigmoid(v)
    return 0.2 * v + 0.8 * v * s, 0.2 + 0.8 * (s + v * s * (1.0 - s))


def three(v):
    return jnp.concatenate([pltpu.roll(v, 1, 1), v, pltpu.roll(v, LANES - 1, 1)], 0).astype(BF)


def fill_columns(out, n, slab, pair, i, j):
    for a in range(3):
        x = 2 * i + a - 1
        tiles = [slab(x, 2 * j - 1), slab(x, 2 * j), slab(x, 2 * j + 1), pair(x, j - 1), pair(x, j)]
        for t, tile in enumerate(tiles):
            row = 80 * a + 16 * t
            out[row : row + 16, n * LANES : (n + 1) * LANES] = tile


def packed(v, step):
    total = None
    for k in range(4):
        part = v[step * k : step * (k + 1)]
        part = jnp.concatenate([part, jnp.zeros((part.shape[0], 96), F32)], 1)
        if part.shape[0] < step:
            part = jnp.concatenate([part, jnp.zeros((step - part.shape[0], LANES), F32)], 0)
        part = pltpu.roll(part, 32 * k, 1) if k else part
        total = part if total is None else total + part
    return total


def forward_kernel(
    f_ref, g_ref, ylo, yhi, xlo, xhi, wd, wm, wg, wb,
    grads_out, slope_out, h2_out, d2_out, up_out, down_out,
    fpair, gpair, h1_three, d2_three, slope, xcol, mcol, gcol, zcol,
):
    def f(x, y):
        if x < 0:
            return xlo[(x + 3) * 13 + y + 3]
        if x > 3:
            return xhi[(x - 4) * 13 + y + 3]
        return ylo[x, y + 3] if y < 0 else yhi[x, y - 8] if y > 7 else f_ref[x, y]

    def g(x, y):
        if x < 0:
            return xlo[39 + y + 1]
        return ylo[x, 3] if y < 0 else g_ref[x, y]

    zero = jnp.zeros((8, LANES), F32)
    for x in range(-3, 6):
        for j in range(-2, 5):
            first = zero if j == -2 else rolled_odd(f(x, 2 * j))
            fpair[x + 3, j + 2] = jnp.concatenate([first, rolled_odd(f(x, 2 * j + 1))], 0).astype(BF)
    for x in range(-1, 4):
        for j in range(-1, 4):
            first = zero if j == -1 else rolled_odd(g(x, 2 * j))
            gpair[x + 1, j + 1] = jnp.concatenate([first, rolled_odd(g(x, 2 * j + 1))], 0).astype(BF)

    def f_pair(x, j):
        return fpair[x + 3, j + 2]

    def g_pair(x, j):
        return gpair[x + 1, j + 1]

    for n, (i, j) in enumerate(LOCAL):
        fill_columns(gcol, n, g, g_pair, i, j)
    for n, (i, j) in enumerate(AROUND):
        fill_columns(xcol, n, f, f_pair, i, j)

    for i in range(-1, 3):
        start = (i + 1) * ROW
        v, s = act_and_slope(dot(wd[...], xcol[:, start : start + ROW]))
        slope[:, start : start + ROW] = s
        for j in range(-1, 5):
            lanes = slice((j + 1) * LANES, (j + 2) * LANES)
            h1_three[i + 1, j + 1] = three(v[:, lanes])
            if i >= 0 and j >= 0:
                slope_out[i * 5 + j] = s[:, lanes]

    for n, (i, j) in enumerate(LOCAL):
        for a in range(3):
            for b in range(3):
                row = 96 * (3 * a + b)
                mcol[row : row + 96, n * LANES : (n + 1) * LANES] = h1_three[i + a, j + b]

    for start in range(0, 8, 4):
        lanes = slice(start * LANES, (start + 4) * LANES)
        v, s = act_and_slope(dot(wm[...], mcol[:, lanes]))
        h2_out[:, lanes] = v.astype(BF)
        d2_out[:, lanes] = (dot(wg[...], gcol[:, lanes]) * s).astype(BF)
    for i in range(2):
        at = 4 * i * LANES
        up_out[i] = d2_out[:, at + 3 * LANES : at + 4 * LANES]
        down_out[i] = d2_out[:, at : at + LANES]
        down_out[2 + i] = d2_out[:, at + LANES : at + 2 * LANES]
        down_out[4 + i] = h2_out[:, at : at + LANES]
    for n, (i, j) in enumerate(LOCAL):
        d2_three[i, j] = three(d2_out[:, n * LANES : (n + 1) * LANES].astype(F32))

    down = jnp.zeros((240, 64), F32)
    for i in range(-1, 3):
        inside = [a for a in range(3) if 0 <= i + a - 1 <= 1]
        depth = 288 * len(inside)
        for m, a in enumerate(inside):
            for b in range(3):
                row = 288 * m + 96 * b
                for j in range(-1, 5):
                    lanes = slice((j + 1) * LANES, (j + 2) * LANES)
                    near = 0 <= j + b - 1 <= 3
                    zcol[row : row + 96, lanes] = d2_three[i + a - 1, j + b - 1] if near else jnp.zeros((96, LANES), BF)
        start = (i + 1) * ROW
        part = dot(wb[i + 1, :, :depth], zcol[:depth]) * slope[:, start : start + ROW]
        high = part.astype(BF)
        low = (part - high.astype(F32)).astype(BF)
        down += dot_nt(xcol[:, start : start + ROW], jnp.concatenate([high, low], 0))
    rows = jnp.concatenate(
        [
            packed(dot_nt(mcol[...], d2_out[...]), 224),
            packed(down[:, :32] + down[:, 32:], 64),
            packed(dot_nt(gcol[...], h2_out[...]), 64),
            jnp.zeros((ROWS - 352, LANES), F32),
        ],
        0,
    )
    grads_out[...] = rows.reshape(grads_out.shape)


def outputs_kernel(
    f_ref, g_ref, h2, d2, ylo, yhi, xlo, xhi, slope, wb, wu, wv,
    mapped_out, grad_out, d2_three, mcol, d1, ucol, slabs,
):
    def d(i, j):
        if i < 0:
            return xlo[j + 1]
        if i > 1:
            return xhi[(i - 2) * 7 + j + 1]
        if j < 0:
            return ylo[i]
        if j > 3:
            return yhi[2 * (j - 4) + i]
        at = (4 * i + j) * LANES
        return d2[:, at : at + LANES]

    for i in range(-1, 4):
        for j in range(-1, 6):
            d2_three[i + 1, j + 1] = three(d(i, j).astype(F32))
    for n, (i, j) in enumerate(UPPER):
        for a in range(3):
            for b in range(3):
                row = 96 * (3 * a + b)
                mcol[row : row + 96, n * LANES : (n + 1) * LANES] = d2_three[i + a, j + b]
    for start in range(0, 15, 4):
        cells = UPPER[start : start + 4]
        v = dot(wb[...], mcol[:, start * LANES : (start + len(cells)) * LANES])
        for n, (i, j) in enumerate(cells):
            at = (start + n) * LANES
            d1[:, at : at + LANES] = (v[:, n * LANES : (n + 1) * LANES] * slope[i * 5 + j]).astype(BF)

    def h(i, j):
        if i > 1:
            return xhi[14 + j]
        if j > 3:
            return yhi[4 + i]
        at = (4 * i + j) * LANES
        return h2[:, at : at + LANES]

    def p(i, j):
        at = UPPER.index((i, j)) * LANES
        return d1[:, at : at + LANES]

    joined = join_z()
    order = slab_order(1)
    for cell, w, base, out in ((h, wu, f_ref, mapped_out), (p, wv, g_ref, grad_out)):
        two = {}
        for i, j in UPPER:
            v = cell(i, j).astype(F32)
            two[i, j] = jnp.concatenate([v, pltpu.roll(v, LANES - 1, 1)], 0).astype(BF)
        for n, (i, j) in enumerate(LOCAL):
            for k in range(4):
                ucol[64 * k : 64 * k + 64, n * LANES : (n + 1) * LANES] = two[i + k // 2, j + k % 2]
        for start in range(0, 8, 2):
            up = dot(w[...], ucol[:, start * LANES : (start + 2) * LANES])
            for n in range(2):
                i, j = LOCAL[start + n]
                for k in range(4):
                    x, y = 2 * i + k // 2, 2 * j + k % 2
                    row = 16 * (8 * x + y)
                    added = base[x, y].astype(F32) + up[16 * k : 16 * k + 16, n * LANES : (n + 1) * LANES]
                    slabs[row : row + 16] = added.astype(BF)
        z = dot(order, slabs[...]).astype(BF)
        out[...] = dot(jnp.concatenate([z[:256], z[256:]], 1), joined).astype(BF)


def tap_rows(rows):
    order = [(0, 1), (0, 2), (1, 1), (1, 2), (2, 1), (2, 2), None, (0, 0), (1, 0), (2, 0)]
    for a in range(3):
        for m, tap in enumerate(order):
            if tap is not None:
                yield 10 * a + m, 9 * a + 3 * tap[0] + tap[1]


def unpack_kernel(total, down_out, mid_out, up_out):
    total = total[...].reshape(ROWS, LANES)
    flipped = jnp.concatenate([total[0:224], jnp.zeros((32, LANES), F32)], 0).T
    for tap in range(27):
        k, m = tap // 7, tap % 7
        rows = flipped[32 * k : 32 * k + 32, LANES * (m // 4) : LANES * (m // 4 + 1)]
        rows = pltpu.roll(rows, LANES - 32 * (m % 4), 1) if m % 4 else rows
        mid_out[tap] = rows[:, :32]
    for k in range(4):
        parts = total[224:352]
        parts = pltpu.roll(parts, LANES - 32 * k, 1) if k else parts
        for block, tap in tap_rows(240):
            if block // 8 == k:
                row = 8 * (block % 8)
                down_out[tap] = parts[row : row + 8, :32]
                up_out[tap] = parts[64 + row : 64 + row + 8, :32]


def down_weights(w):
    none = jnp.zeros_like(w[:, 0, 0])
    blocks = [w[:, 0, 1], w[:, 0, 2], w[:, 1, 1], w[:, 1, 2], w[:, 2, 1], w[:, 2, 2], none, w[:, 0, 0], w[:, 1, 0], w[:, 2, 0]]
    return jnp.transpose(jnp.stack(blocks, 1), (2, 0, 1, 3)).reshape(32, 240)


def up_weights(w):
    none = jnp.zeros_like(w[0, 0, 0])
    pick = ((1, None), (2, 0))
    rows = []
    for p in range(2):
        for q in range(2):
            for r in range(2):
                row = []
                for k in range(8):
                    a, b, d = pick[p][k // 4], pick[q][k // 2 % 2], pick[r][k % 2]
                    row.append(none if None in (a, b, d) else w[a, b, d])
                rows.append(jnp.concatenate(row, 1))
    return jnp.concatenate(rows, 0)


def all_sum(part):
    def spread(x, axes):
        return jnp.broadcast_to(x[None], (lax.axis_size(axes),) + x.shape)

    part = lax.all_to_all(part, ("x", "core"), 0, 0, tiled=True).sum(0)
    for axes in (("z",), ("yl", "yh")):
        part = lax.all_to_all(spread(part, axes), axes, 0, 0, tiled=True).sum(0)
    return lax.all_to_all(spread(part, ("x", "core")), ("x", "core"), 0, 0, tiled=True)


def local(fields, cotangent, w_down, w_mid, w_up):
    w_down_swapped = jnp.swapaxes(w_down, 3, 4)
    wd = down_weights(w_down)
    wg = down_weights(jnp.swapaxes(w_up, 3, 4))
    wm = jnp.transpose(w_mid, (3, 0, 1, 2, 4)).reshape(32, 864)
    wb = jnp.transpose(w_mid[::-1, ::-1, ::-1], (4, 0, 1, 2, 3)).reshape(32, 864)
    none = jnp.zeros((32, 288), BF)
    wb_rows = jnp.stack([jnp.concatenate([wb[:, 576:], none], 1), wb[:, 288:], wb[:, :576], jnp.concatenate([wb[:, :288], none], 1)], 0)
    wu = up_weights(w_up)
    wv = up_weights(w_down_swapped)

    f, g, up, down = call(
        to_slabs_kernel,
        [((4, 8, 16, LANES), BF)] * 2 + [((4, 4, 16, LANES), BF), ((4, 2, 16, LANES), BF)],
        [fields.reshape(256, 256), cotangent.reshape(256, 256)],
        [((2, 256, 256), BF), pltpu.SemaphoreType.DMA((2,))],
        space=pl.ANY,
    )
    ylo, yhi = shift(up, GY, 1), shift(down, GY, -1)
    f_ext = jnp.concatenate([ylo[:, :3], f, yhi], 1)
    last = jnp.concatenate([f_ext[1:].reshape(39, 16, LANES), ylo[3, 3:4], g[3]], 0)
    xlo = shift(last, GX, 1)
    xhi = shift(f_ext[:2].reshape(26, 16, LANES), GX, -1)

    parts = lax.axis_size(("x", "core"))
    grads, slope, h2, d2, up, down = call(
        forward_kernel,
        [((parts, ROWS // parts, LANES), F32), ((15, 32, LANES), F32), ((32, 8 * LANES), BF), ((32, 8 * LANES), BF),
         ((2, 32, LANES), BF), ((6, 32, LANES), BF)],
        [f, g, ylo, yhi, xlo, xhi, wd, wm, wg, wb_rows],
        [((9, 7, 16, LANES), BF), ((5, 5, 16, LANES), BF), ((4, 6, 96, LANES), BF), ((2, 4, 96, LANES), BF),
         ((32, 4 * ROW), F32), ((240, 4 * ROW), BF), ((864, 8 * LANES), BF), ((240, 8 * LANES), BF), ((576, ROW), BF)],
    )
    ylo, yhi = shift(up, GY, 1), shift(down, GY, -1)
    cells = jnp.transpose(d2.reshape(32, 8, LANES), (1, 0, 2))
    last = jnp.concatenate([ylo[1:2], cells[4:8], yhi[1:2], yhi[3:4]], 0)
    first = jnp.concatenate(
        [ylo[0:1], cells[0:4], yhi[0:1], yhi[2:3], last]
        + [h2[None, :, j * LANES : (j + 1) * LANES] for j in range(4)] + [yhi[4:5]], 0
    )
    xlo = shift(last, GX, 1)
    xhi = shift(first, GX, -1)

    mapped, grad_fields = call(
        outputs_kernel,
        [((256, 256), BF)] * 2,
        [f, g, h2, d2, ylo, yhi, xlo, xhi, slope, wb, wu, wv],
        [((5, 7, 96, LANES), BF), ((864, 15 * LANES), BF), ((32, 15 * LANES), BF), ((256, 8 * LANES), BF), ((512, LANES), BF)],
    )
    grad_down, grad_mid, grad_up = call(
        unpack_kernel,
        [((27, 8, 32), F32), ((27, 32, 32), F32), ((27, 8, 32), F32)],
        [all_sum(grads)],
    )
    return (
        mapped.reshape(fields.shape),
        grad_fields.reshape(fields.shape),
        jnp.swapaxes(grad_down.reshape(w_down_swapped.shape), 3, 4),
        grad_mid.reshape(w_mid.shape),
        grad_up.reshape(w_up.shape),
    )


def solution(mesh):
    nx, ny = mesh.devices.shape
    fine = Mesh(mesh.devices.reshape(nx // 4, 4, ny // 4, 2, 2), GX + GY)
    block = P(None, GX, GY, None)
    specs = (block, block, P(), P(), P())
    return jax.shard_map(local, mesh=fine, in_specs=specs, out_specs=specs, check_vma=False)
```

```python
import jax
import jax.numpy as jnp
from jax import lax
from jax.experimental import pallas as pl
from jax.experimental.pallas import tpu as pltpu
from jax.sharding import Mesh
from jax.sharding import PartitionSpec as P

BF = jnp.bfloat16
F32 = jnp.float32
LANES = 128
LOCAL = [(i, j) for i in range(2) for j in range(4)]
UPPER = LOCAL + [(0, 4), (1, 4)] + [(2, j) for j in range(5)]
WIDE = LOCAL + [(i, j) for j in (-1, 4, 5) for i in range(2)]
AROUND = [(i, j) for i in range(-1, 3) for j in range(-2, 7)]
ROW = 9 * LANES
ROWS = 384
GX = ("z", "yl")
GY = ("x", "yh", "core")
XC, Y, Z = ("x", "core"), ("yl", "yh"), ("z",)


def shift(x, axis, by):
    devices = lax.axis_size(axis)
    return lax.ppermute(x, axis, [(i, (i + by) % devices) for i in range(devices)])


def call(body, outs, args, scratch=(), after=()):
    moved = 2 * 10**6
    flops = 10**8
    return pl.pallas_call(
        body,
        out_shape=[jax.ShapeDtypeStruct(s, d) for s, d in outs],
        in_specs=[pl.BlockSpec(memory_space=pltpu.VMEM)] * len(args) + [pl.BlockSpec(memory_space=pl.ANY)] * len(after),
        out_specs=[pl.BlockSpec(memory_space=pltpu.VMEM)] * len(outs),
        scratch_shapes=[pltpu.VMEM(*s) for s in scratch],
        compiler_params=pltpu.CompilerParams(vmem_limit_bytes=32 * 2**20),
        cost_estimate=pl.CostEstimate(flops=flops, bytes_accessed=moved, transcendentals=0),
    )(*args, *after)


def dot(a, b):
    return lax.dot_general(a, b, (((1,), (0,)), ((), ())), preferred_element_type=F32)


def dot_nt(a, b):
    return lax.dot_general(a, b, (((1,), (1,)), ((), ())), preferred_element_type=F32)


def split_z():
    z = lax.broadcasted_iota(jnp.int32, (256, 256), 0)
    k = lax.broadcasted_iota(jnp.int32, (256, 256), 1)
    return (z == 2 * (k & 127) + (k >> 7)).astype(F32).astype(BF)


def join_z():
    k = lax.broadcasted_iota(jnp.int32, (256, 256), 0)
    z = lax.broadcasted_iota(jnp.int32, (256, 256), 1)
    return (z == 2 * (k & 127) + (k >> 7)).astype(F32).astype(BF)


def slab_order(dim):
    r = lax.broadcasted_iota(jnp.int32, (512, 512), dim)
    s = lax.broadcasted_iota(jnp.int32, (512, 512), 1 - dim)
    source = ((r >> 3) & 1) * 256 + (r & 7) * 32 + (r >> 7) * 8 + ((r >> 4) & 7)
    return (s == source).astype(F32).astype(BF)


def to_slabs_kernel(f_ref, g_ref, f_out, g_out, up_out, down_out):
    halves = split_z()
    order = slab_order(0)
    for ref, out in ((f_ref, f_out), (g_ref, g_out)):
        z = dot(ref[...], halves).astype(BF)
        z = jnp.concatenate([z[:, :LANES], z[:, LANES:]], 0)
        out[...] = dot(order, z).astype(BF).reshape(4, 8, 16, LANES)
    up_out[:, 0:5] = f_out[:, 3:8]
    up_out[:, 5:8] = g_out[:, 5:8]
    down_out[:, 0:6] = f_out[:, 0:6]
    down_out[:, 6:10] = g_out[:, 0:4]


def rolled_odd(slab):
    return pltpu.roll(slab.astype(F32)[8:], 1, 1)


def act_and_slope(v):
    s = jax.nn.sigmoid(v)
    return 0.2 * v + 0.8 * v * s, 0.2 + 0.8 * (s + v * s * (1.0 - s))


def three(v):
    return jnp.concatenate([pltpu.roll(v, 1, 1), v, pltpu.roll(v, LANES - 1, 1)], 0).astype(BF)


def fill_columns(out, n, slab, pair, i, j):
    for a in range(3):
        x = 2 * i + a - 1
        tiles = [slab(x, 2 * j - 1), slab(x, 2 * j), slab(x, 2 * j + 1), pair(x, j - 1), pair(x, j)]
        for t, tile in enumerate(tiles):
            row = 80 * a + 16 * t
            out[row : row + 16, n * LANES : (n + 1) * LANES] = tile


def packed(v, step):
    total = None
    for k in range(4):
        part = v[step * k : step * (k + 1)]
        part = jnp.concatenate([part, jnp.zeros((part.shape[0], 96), F32)], 1)
        if part.shape[0] < step:
            part = jnp.concatenate([part, jnp.zeros((step - part.shape[0], LANES), F32)], 0)
        part = pltpu.roll(part, 32 * k, 1) if k else part
        total = part if total is None else total + part
    return total


def forward_kernel(
    f_ref, g_ref, ylo, yhi, xlo, xhi, wd, wm, wg, wb,
    grads_out, slope_out, h2_out, d2_out,
    fpair, gpair, h1_three, d2_three, slope, xcol, mcol, gcol, zcol,
):
    def f(x, y):
        if x < 0:
            return xlo[(x + 3) * 19 + y + 5]
        if x > 3:
            return xhi[(x - 4) * 19 + y + 5]
        return ylo[x, y + 5] if y < 0 else yhi[x, y - 8] if y > 7 else f_ref[x, y]

    def g(x, y):
        if x < 0:
            return xlo[57 + y + 3]
        return ylo[x, 5 + y + 3] if y < 0 else yhi[x, 6 + y - 8] if y > 7 else g_ref[x, y]

    zero = jnp.zeros((8, LANES), F32)
    for x in range(-3, 6):
        for j in range(-3, 7):
            first = zero if j == -3 else rolled_odd(f(x, 2 * j))
            fpair[x + 3, j + 3] = jnp.concatenate([first, rolled_odd(f(x, 2 * j + 1))], 0).astype(BF)
    for x in range(-1, 4):
        for j in range(-2, 6):
            first = zero if j == -2 else rolled_odd(g(x, 2 * j))
            gpair[x + 1, j + 2] = jnp.concatenate([first, rolled_odd(g(x, 2 * j + 1))], 0).astype(BF)

    def f_pair(x, j):
        return fpair[x + 3, j + 3]

    def g_pair(x, j):
        return gpair[x + 1, j + 2]

    for n, (i, j) in enumerate(WIDE):
        fill_columns(gcol, n, g, g_pair, i, j)
    for n, (i, j) in enumerate(AROUND):
        fill_columns(xcol, n, f, f_pair, i, j)

    for i in range(-1, 3):
        start = (i + 1) * ROW
        v, s = act_and_slope(dot(wd[...], xcol[:, start : start + ROW]))
        slope[:, start : start + ROW] = s
        for j in range(-2, 7):
            lanes = slice((j + 2) * LANES, (j + 3) * LANES)
            h1_three[i + 1, j + 2] = three(v[:, lanes])
            if i >= 0 and 0 <= j <= 4:
                slope_out[i * 5 + j] = s[:, lanes]

    for n, (i, j) in enumerate(WIDE):
        for a in range(3):
            for b in range(3):
                row = 96 * (3 * a + b)
                mcol[row : row + 96, n * LANES : (n + 1) * LANES] = h1_three[i + a, j + b + 1]

    for start in range(0, 14, 7):
        lanes = slice(start * LANES, (start + 7) * LANES)
        v, s = act_and_slope(dot(wm[...], mcol[:, lanes]))
        h2_out[:, lanes] = v.astype(BF)
        d2_out[:, lanes] = (dot(wg[...], gcol[:, lanes]) * s).astype(BF)
    for n, (i, j) in enumerate(LOCAL):
        d2_three[i, j] = three(d2_out[:, n * LANES : (n + 1) * LANES].astype(F32))

    down = jnp.zeros((240, 64), F32)
    for i in range(-1, 3):
        inside = [a for a in range(3) if 0 <= i + a - 1 <= 1]
        depth = 288 * len(inside)
        for m, a in enumerate(inside):
            for b in range(3):
                row = 288 * m + 96 * b
                for j in range(-1, 5):
                    lanes = slice((j + 1) * LANES, (j + 2) * LANES)
                    near = 0 <= j + b - 1 <= 3
                    zcol[row : row + 96, lanes] = d2_three[i + a - 1, j + b - 1] if near else jnp.zeros((96, LANES), BF)
        start = (i + 1) * ROW + LANES
        part = dot(wb[i + 1, :, :depth], zcol[:depth]) * slope[:, start : start + 6 * LANES]
        high = part.astype(BF)
        low = (part - high.astype(F32)).astype(BF)
        down += dot_nt(xcol[:, start : start + 6 * LANES], jnp.concatenate([high, low], 0))
    rows = jnp.concatenate(
        [
            packed(dot_nt(mcol[:, : 8 * LANES], d2_out[:, : 8 * LANES]), 224),
            packed(down[:, :32] + down[:, 32:], 64),
            packed(dot_nt(gcol[:, : 8 * LANES], h2_out[:, : 8 * LANES]), 64),
            jnp.zeros((ROWS - 352, LANES), F32),
        ],
        0,
    )
    grads_out[...] = rows.reshape(grads_out.shape)


def cell_of(ref, i, j):
    at = WIDE.index((i, j)) * LANES
    return ref[:, at : at + LANES]


def x_rows_kernel(h2, d2, after, up_out, down_out):
    for j in range(7):
        up_out[j] = cell_of(d2, 1, j - 1)
        down_out[j] = cell_of(d2, 0, j - 1)
        down_out[7 + j] = cell_of(d2, 1, j - 1)
    for j in range(5):
        down_out[14 + j] = cell_of(h2, 0, j)


def outputs_kernel(
    f_ref, g_ref, h2, d2, xlo, xhi, slope, wb, wu, wv, after,
    mapped_out, grad_out, d2_three, mcol, d1, ucol, slabs,
):
    def d(i, j):
        if i < 0:
            return xlo[j + 1]
        if i > 1:
            return xhi[(i - 2) * 7 + j + 1]
        return cell_of(d2, i, j)

    for i in range(-1, 4):
        for j in range(-1, 6):
            d2_three[i + 1, j + 1] = three(d(i, j).astype(F32))
    for n, (i, j) in enumerate(UPPER):
        for a in range(3):
            for b in range(3):
                row = 96 * (3 * a + b)
                mcol[row : row + 96, n * LANES : (n + 1) * LANES] = d2_three[i + a, j + b]
    for start in range(0, 15, 4):
        cells = UPPER[start : start + 4]
        v = dot(wb[...], mcol[:, start * LANES : (start + len(cells)) * LANES])
        for n, (i, j) in enumerate(cells):
            at = (start + n) * LANES
            d1[:, at : at + LANES] = (v[:, n * LANES : (n + 1) * LANES] * slope[i * 5 + j]).astype(BF)

    def h(i, j):
        if i > 1:
            return xhi[14 + j]
        return cell_of(h2, i, j)

    def p(i, j):
        at = UPPER.index((i, j)) * LANES
        return d1[:, at : at + LANES]

    joined = join_z()
    order = slab_order(1)
    for cell, w, base, out in ((h, wu, f_ref, mapped_out), (p, wv, g_ref, grad_out)):
        two = {}
        for i, j in UPPER:
            v = cell(i, j).astype(F32)
            two[i, j] = jnp.concatenate([v, pltpu.roll(v, LANES - 1, 1)], 0).astype(BF)
        for n, (i, j) in enumerate(LOCAL):
            for k in range(4):
                ucol[64 * k : 64 * k + 64, n * LANES : (n + 1) * LANES] = two[i + k // 2, j + k % 2]
        for start in range(0, 8, 2):
            up = dot(w[...], ucol[:, start * LANES : (start + 2) * LANES])
            for n in range(2):
                i, j = LOCAL[start + n]
                for k in range(4):
                    x, y = 2 * i + k // 2, 2 * j + k % 2
                    row = 16 * (8 * x + y)
                    added = base[x, y].astype(F32) + up[16 * k : 16 * k + 16, n * LANES : (n + 1) * LANES]
                    slabs[row : row + 16] = added.astype(BF)
        z = dot(order, slabs[...]).astype(BF)
        out[...] = dot(jnp.concatenate([z[:256], z[256:]], 1), joined).astype(BF)


def tap_rows(rows):
    order = [(0, 1), (0, 2), (1, 1), (1, 2), (2, 1), (2, 2), None, (0, 0), (1, 0), (2, 0)]
    for a in range(3):
        for m, tap in enumerate(order):
            if tap is not None:
                yield 10 * a + m, 9 * a + 3 * tap[0] + tap[1]


def unpack_kernel(total, down_out, mid_out, up_out):
    total = total[...].reshape(ROWS, LANES)
    flipped = jnp.concatenate([total[0:224], jnp.zeros((32, LANES), F32)], 0).T
    for tap in range(27):
        k, m = tap // 7, tap % 7
        rows = flipped[32 * k : 32 * k + 32, LANES * (m // 4) : LANES * (m // 4 + 1)]
        rows = pltpu.roll(rows, LANES - 32 * (m % 4), 1) if m % 4 else rows
        mid_out[tap] = rows[:, :32]
    for k in range(4):
        parts = total[224:352]
        parts = pltpu.roll(parts, LANES - 32 * k, 1) if k else parts
        for block, tap in tap_rows(240):
            if block // 8 == k:
                row = 8 * (block % 8)
                down_out[tap] = parts[row : row + 8, :32]
                up_out[tap] = parts[64 + row : 64 + row + 8, :32]


def down_weights(w):
    none = jnp.zeros_like(w[:, 0, 0])
    blocks = [w[:, 0, 1], w[:, 0, 2], w[:, 1, 1], w[:, 1, 2], w[:, 2, 1], w[:, 2, 2], none, w[:, 0, 0], w[:, 1, 0], w[:, 2, 0]]
    return jnp.transpose(jnp.stack(blocks, 1), (2, 0, 1, 3)).reshape(32, 240)


def up_weights(w):
    none = jnp.zeros_like(w[0, 0, 0])
    pick = ((1, None), (2, 0))
    rows = []
    for p in range(2):
        for q in range(2):
            for r in range(2):
                row = []
                for k in range(8):
                    a, b, d = pick[p][k // 4], pick[q][k // 2 % 2], pick[r][k % 2]
                    row.append(none if None in (a, b, d) else w[a, b, d])
                rows.append(jnp.concatenate(row, 1))
    return jnp.concatenate(rows, 0)


def exchange(part, axes):
    return lax.all_to_all(part, axes, 0, 0, tiled=True)


def sum_kernel(got, *refs):
    refs[-1][...] = jnp.broadcast_to(jnp.sum(got[...], 0, keepdims=True), refs[-1].shape)


def sum_spread(got, axes, after=()):
    return call(sum_kernel, [((lax.axis_size(axes),) + got.shape[1:], F32)], [got], after=after)[0]


def local(fields, cotangent, w_down, w_mid, w_up):
    w_down_swapped = jnp.swapaxes(w_down, 3, 4)
    wd = down_weights(w_down)
    wg = down_weights(jnp.swapaxes(w_up, 3, 4))
    wm = jnp.transpose(w_mid, (3, 0, 1, 2, 4)).reshape(32, 864)
    wb = jnp.transpose(w_mid[::-1, ::-1, ::-1], (4, 0, 1, 2, 3)).reshape(32, 864)
    none = jnp.zeros((32, 288), BF)
    wb_rows = jnp.stack([jnp.concatenate([wb[:, 576:], none], 1), wb[:, 288:], wb[:, :576], jnp.concatenate([wb[:, :288], none], 1)], 0)
    wu = up_weights(w_up)
    wv = up_weights(w_down_swapped)

    f, g, up, down = call(
        to_slabs_kernel,
        [((4, 8, 16, LANES), BF)] * 2 + [((4, 8, 16, LANES), BF), ((4, 10, 16, LANES), BF)],
        [fields.reshape(256, 256), cotangent.reshape(256, 256)],
    )
    ylo, yhi = shift(up, GY, 1), shift(down, GY, -1)
    f_ext = jnp.concatenate([ylo[:, :5], f, yhi[:, :6]], 1)
    last = jnp.concatenate([f_ext[1:].reshape(57, 16, LANES), ylo[3, 5:], g[3], yhi[3, 6:]], 0)
    xlo = shift(last, GX, 1)
    xhi = shift(f_ext[:2].reshape(38, 16, LANES), GX, -1)

    parts = lax.axis_size(XC)
    grads, slope, h2, d2 = call(
        forward_kernel,
        [((parts, ROWS // parts, LANES), F32), ((15, 32, LANES), F32), ((32, 14 * LANES), BF), ((32, 14 * LANES), BF)],
        [f, g, ylo, yhi, xlo, xhi, wd, wm, wg, wb_rows],
        [((9, 10, 16, LANES), BF), ((5, 8, 16, LANES), BF), ((4, 9, 96, LANES), BF), ((2, 4, 96, LANES), BF),
         ((32, 4 * ROW), F32), ((240, 4 * ROW), BF), ((864, 14 * LANES), BF), ((240, 14 * LANES), BF),
         ((576, 6 * LANES), BF)],
    )

    got = exchange(grads, XC)
    last, first = call(x_rows_kernel, [((7, 32, LANES), BF), ((19, 32, LANES), BF)], [h2, d2], after=[got])
    xlo, xhi = shift(last, GX, 1), shift(first, GX, -1)
    got = exchange(sum_spread(got, Z), Z)
    got = exchange(sum_spread(got, Y, after=[xlo, xhi]), Y)
    mapped, grad_fields = call(
        outputs_kernel,
        [((256, 256), BF)] * 2,
        [f, g, h2, d2, xlo, xhi, slope, wb, wu, wv],
        [((5, 7, 96, LANES), BF), ((864, 15 * LANES), BF), ((32, 15 * LANES), BF), ((256, 8 * LANES), BF), ((512, LANES), BF)],
        after=[got],
    )
    grad_down, grad_mid, grad_up = call(
        unpack_kernel,
        [((27, 8, 32), F32), ((27, 32, 32), F32), ((27, 8, 32), F32)],
        [exchange(sum_spread(got, XC), XC)],
    )
    return (
        mapped.reshape(fields.shape),
        grad_fields.reshape(fields.shape),
        jnp.swapaxes(grad_down.reshape(w_down_swapped.shape), 3, 4),
        grad_mid.reshape(w_mid.shape),
        grad_up.reshape(w_up.shape),
    )


def solution(mesh):
    nx, ny = mesh.devices.shape
    fine = Mesh(mesh.devices.reshape(nx // 4, 4, ny // 4, 2, 2), GX + GY)
    block = P(None, GX, GY, None)
    specs = (block, block, P(), P(), P())
    return jax.shard_map(local, mesh=fine, in_specs=specs, out_specs=specs, check_vma=False)
```

```python
import jax
import jax.numpy as jnp
from jax import lax
from jax.experimental import pallas as pl
from jax.experimental.pallas import tpu as pltpu
from jax.sharding import Mesh
from jax.sharding import PartitionSpec as P

BF = jnp.bfloat16
F32 = jnp.float32
LANES = 128
LOCAL = [(i, j) for i in range(2) for j in range(4)]
UPPER = LOCAL + [(0, 4), (1, 4)] + [(2, j) for j in range(5)]
WIDE = LOCAL + [(i, j) for j in (-1, 4, 5) for i in range(2)]
AROUND = [(i, j) for i in range(-1, 3) for j in range(-2, 7)]
ROW = 9 * LANES
ROWS = 384
GX = ("z", "yl")
GY = ("x", "yh", "core")
XC, Y, Z = ("x", "core"), ("yl", "yh"), ("z",)


def shift(x, axis, by):
    devices = lax.axis_size(axis)
    return lax.ppermute(x, axis, [(i, (i + by) % devices) for i in range(devices)])


def call(body, outs, args, scratch=(), after=(), flops=10**8):
    moved = 2 * 10**6
    return pl.pallas_call(
        body,
        out_shape=[jax.ShapeDtypeStruct(s, d) for s, d in outs],
        in_specs=[pl.BlockSpec(memory_space=pltpu.VMEM)] * len(args) + [pl.BlockSpec(memory_space=pl.ANY)] * len(after),
        out_specs=[pl.BlockSpec(memory_space=pltpu.VMEM)] * len(outs),
        scratch_shapes=[pltpu.VMEM(*s) for s in scratch],
        compiler_params=pltpu.CompilerParams(vmem_limit_bytes=32 * 2**20),
        cost_estimate=pl.CostEstimate(flops=flops, bytes_accessed=moved, transcendentals=0),
    )(*args, *after)


def dot(a, b):
    return lax.dot_general(a, b, (((1,), (0,)), ((), ())), preferred_element_type=F32)


def dot_nt(a, b):
    return lax.dot_general(a, b, (((1,), (1,)), ((), ())), preferred_element_type=F32)


def split_z():
    z = lax.broadcasted_iota(jnp.int32, (256, 256), 0)
    k = lax.broadcasted_iota(jnp.int32, (256, 256), 1)
    return (z == 2 * (k & 127) + (k >> 7)).astype(F32).astype(BF)


def join_z():
    k = lax.broadcasted_iota(jnp.int32, (256, 256), 0)
    z = lax.broadcasted_iota(jnp.int32, (256, 256), 1)
    return (z == 2 * (k & 127) + (k >> 7)).astype(F32).astype(BF)


def slab_order(dim):
    r = lax.broadcasted_iota(jnp.int32, (512, 512), dim)
    s = lax.broadcasted_iota(jnp.int32, (512, 512), 1 - dim)
    source = ((r >> 3) & 1) * 256 + (r & 7) * 32 + (r >> 7) * 8 + ((r >> 4) & 7)
    return (s == source).astype(F32).astype(BF)


def to_slabs_kernel(f_ref, g_ref, f_out, g_out, up_out, down_out):
    halves = split_z()
    order = slab_order(0)
    for ref, out in ((f_ref, f_out), (g_ref, g_out)):
        z = dot(ref[...], halves).astype(BF)
        z = jnp.concatenate([z[:, :LANES], z[:, LANES:]], 0)
        out[...] = dot(order, z).astype(BF).reshape(4, 8, 16, LANES)
    up_out[:, 0:5] = f_out[:, 3:8]
    up_out[:, 5:8] = g_out[:, 5:8]
    down_out[:, 0:6] = f_out[:, 0:6]
    down_out[:, 6:10] = g_out[:, 0:4]


def rolled_odd(slab):
    return pltpu.roll(slab.astype(F32)[8:], 1, 1)


def act_and_slope(v):
    s = jax.nn.sigmoid(v)
    return 0.2 * v + 0.8 * v * s, 0.2 + 0.8 * (s + v * s * (1.0 - s))


def three(v):
    return jnp.concatenate([pltpu.roll(v, 1, 1), v, pltpu.roll(v, LANES - 1, 1)], 0).astype(BF)


def fill_columns(out, n, slab, pair, i, j):
    for a in range(3):
        x = 2 * i + a - 1
        tiles = [slab(x, 2 * j - 1), slab(x, 2 * j), slab(x, 2 * j + 1), pair(x, j - 1), pair(x, j)]
        for t, tile in enumerate(tiles):
            row = 80 * a + 16 * t
            out[row : row + 16, n * LANES : (n + 1) * LANES] = tile


def packed(v, step):
    total = None
    for k in range(4):
        part = v[step * k : step * (k + 1)]
        part = jnp.concatenate([part, jnp.zeros((part.shape[0], 96), F32)], 1)
        if part.shape[0] < step:
            part = jnp.concatenate([part, jnp.zeros((step - part.shape[0], LANES), F32)], 0)
        part = pltpu.roll(part, 32 * k, 1) if k else part
        total = part if total is None else total + part
    return total


def forward_kernel(
    f_ref, g_ref, ylo, yhi, xlo, xhi, wd, wm, wg, wb,
    grads_out, slope_out, h2_out, d2_out,
    fpair, gpair, h1_three, d2_three, slope, xcol, mcol, gcol, zcol,
):
    def f(x, y):
        if x < 0:
            return xlo[(x + 3) * 19 + y + 5]
        if x > 3:
            return xhi[(x - 4) * 19 + y + 5]
        return ylo[x, y + 5] if y < 0 else yhi[x, y - 8] if y > 7 else f_ref[x, y]

    def g(x, y):
        if x < 0:
            return xlo[57 + y + 3]
        return ylo[x, 5 + y + 3] if y < 0 else yhi[x, 6 + y - 8] if y > 7 else g_ref[x, y]

    zero = jnp.zeros((8, LANES), F32)
    for x in range(-3, 6):
        for j in range(-3, 7):
            first = zero if j == -3 else rolled_odd(f(x, 2 * j))
            fpair[x + 3, j + 3] = jnp.concatenate([first, rolled_odd(f(x, 2 * j + 1))], 0).astype(BF)
    for x in range(-1, 4):
        for j in range(-2, 6):
            first = zero if j == -2 else rolled_odd(g(x, 2 * j))
            gpair[x + 1, j + 2] = jnp.concatenate([first, rolled_odd(g(x, 2 * j + 1))], 0).astype(BF)

    def f_pair(x, j):
        return fpair[x + 3, j + 3]

    def g_pair(x, j):
        return gpair[x + 1, j + 2]

    for n, (i, j) in enumerate(WIDE):
        fill_columns(gcol, n, g, g_pair, i, j)
    for n, (i, j) in enumerate(AROUND):
        fill_columns(xcol, n, f, f_pair, i, j)

    for i in range(-1, 3):
        start = (i + 1) * ROW
        v, s = act_and_slope(dot(wd[...], xcol[:, start : start + ROW]))
        slope[:, start : start + ROW] = s
        for j in range(-2, 7):
            lanes = slice((j + 2) * LANES, (j + 3) * LANES)
            h1_three[i + 1, j + 2] = three(v[:, lanes])
            if i >= 0 and 0 <= j <= 4:
                slope_out[i * 5 + j] = s[:, lanes]

    for n, (i, j) in enumerate(WIDE):
        for a in range(3):
            for b in range(3):
                row = 96 * (3 * a + b)
                mcol[row : row + 96, n * LANES : (n + 1) * LANES] = h1_three[i + a, j + b + 1]

    for start in range(0, 14, 7):
        lanes = slice(start * LANES, (start + 7) * LANES)
        v, s = act_and_slope(dot(wm[...], mcol[:, lanes]))
        h2_out[:, lanes] = v.astype(BF)
        d2_out[:, lanes] = (dot(wg[...], gcol[:, lanes]) * s).astype(BF)
    for n, (i, j) in enumerate(LOCAL):
        d2_three[i, j] = three(d2_out[:, n * LANES : (n + 1) * LANES].astype(F32))

    down = jnp.zeros((240, 64), F32)
    for i in range(-1, 3):
        inside = [a for a in range(3) if 0 <= i + a - 1 <= 1]
        depth = 288 * len(inside)
        for m, a in enumerate(inside):
            for b in range(3):
                row = 288 * m + 96 * b
                for j in range(-1, 5):
                    lanes = slice((j + 1) * LANES, (j + 2) * LANES)
                    near = 0 <= j + b - 1 <= 3
                    zcol[row : row + 96, lanes] = d2_three[i + a - 1, j + b - 1] if near else jnp.zeros((96, LANES), BF)
        start = (i + 1) * ROW + LANES
        part = dot(wb[i + 1, :, :depth], zcol[:depth]) * slope[:, start : start + 6 * LANES]
        high = part.astype(BF)
        low = (part - high.astype(F32)).astype(BF)
        down += dot_nt(xcol[:, start : start + 6 * LANES], jnp.concatenate([high, low], 0))
    rows = jnp.concatenate(
        [
            packed(dot_nt(mcol[:, : 8 * LANES], d2_out[:, : 8 * LANES]), 224),
            packed(down[:, :32] + down[:, 32:], 64),
            packed(dot_nt(gcol[:, : 8 * LANES], h2_out[:, : 8 * LANES]), 64),
            jnp.zeros((ROWS - 352, LANES), F32),
        ],
        0,
    )
    grads_out[...] = rows.reshape(grads_out.shape)


def cell_of(ref, i, j):
    at = WIDE.index((i, j)) * LANES
    return ref[:, at : at + LANES]


def x_rows_kernel(h2, d2, after, up_out, down_out):
    for j in range(7):
        up_out[j] = cell_of(d2, 1, j - 1)
        down_out[j] = cell_of(d2, 0, j - 1)
        down_out[7 + j] = cell_of(d2, 1, j - 1)
    for j in range(5):
        down_out[14 + j] = cell_of(h2, 0, j)


def outputs_kernel(
    f_ref, g_ref, h2, d2, xlo, xhi, slope, wb, wu, wv,
    mapped_out, grad_out, d2_three, mcol, d1, ucol, slabs,
):
    def d(i, j):
        if i < 0:
            return xlo[j + 1]
        if i > 1:
            return xhi[(i - 2) * 7 + j + 1]
        return cell_of(d2, i, j)

    for i in range(-1, 4):
        for j in range(-1, 6):
            d2_three[i + 1, j + 1] = three(d(i, j).astype(F32))
    for n, (i, j) in enumerate(UPPER):
        for a in range(3):
            for b in range(3):
                row = 96 * (3 * a + b)
                mcol[row : row + 96, n * LANES : (n + 1) * LANES] = d2_three[i + a, j + b]
    for start in range(0, 15, 4):
        cells = UPPER[start : start + 4]
        v = dot(wb[...], mcol[:, start * LANES : (start + len(cells)) * LANES])
        for n, (i, j) in enumerate(cells):
            at = (start + n) * LANES
            d1[:, at : at + LANES] = (v[:, n * LANES : (n + 1) * LANES] * slope[i * 5 + j]).astype(BF)

    def h(i, j):
        if i > 1:
            return xhi[14 + j]
        return cell_of(h2, i, j)

    def p(i, j):
        at = UPPER.index((i, j)) * LANES
        return d1[:, at : at + LANES]

    joined = join_z()
    order = slab_order(1)
    for cell, w, base, out in ((h, wu, f_ref, mapped_out), (p, wv, g_ref, grad_out)):
        two = {}
        for i, j in UPPER:
            v = cell(i, j).astype(F32)
            two[i, j] = jnp.concatenate([v, pltpu.roll(v, LANES - 1, 1)], 0).astype(BF)
        for n, (i, j) in enumerate(LOCAL):
            for k in range(4):
                ucol[64 * k : 64 * k + 64, n * LANES : (n + 1) * LANES] = two[i + k // 2, j + k % 2]
        for start in range(0, 8, 2):
            up = dot(w[...], ucol[:, start * LANES : (start + 2) * LANES])
            for n in range(2):
                i, j = LOCAL[start + n]
                for k in range(4):
                    x, y = 2 * i + k // 2, 2 * j + k % 2
                    row = 16 * (8 * x + y)
                    added = base[x, y].astype(F32) + up[16 * k : 16 * k + 16, n * LANES : (n + 1) * LANES]
                    slabs[row : row + 16] = added.astype(BF)
        z = dot(order, slabs[...]).astype(BF)
        out[...] = dot(jnp.concatenate([z[:256], z[256:]], 1), joined).astype(BF)


def tap_rows(rows):
    order = [(0, 1), (0, 2), (1, 1), (1, 2), (2, 1), (2, 2), None, (0, 0), (1, 0), (2, 0)]
    for a in range(3):
        for m, tap in enumerate(order):
            if tap is not None:
                yield 10 * a + m, 9 * a + 3 * tap[0] + tap[1]


def unpack_kernel(total, down_out, mid_out, up_out):
    total = total[...].astype(F32).reshape(ROWS, LANES)
    flipped = jnp.concatenate([total[0:224], jnp.zeros((32, LANES), F32)], 0).T
    for tap in range(27):
        k, m = tap // 7, tap % 7
        rows = flipped[32 * k : 32 * k + 32, LANES * (m // 4) : LANES * (m // 4 + 1)]
        rows = pltpu.roll(rows, LANES - 32 * (m % 4), 1) if m % 4 else rows
        mid_out[tap] = rows[:, :32]
    for k in range(4):
        parts = total[224:352]
        parts = pltpu.roll(parts, LANES - 32 * k, 1) if k else parts
        for block, tap in tap_rows(240):
            if block // 8 == k:
                row = 8 * (block % 8)
                down_out[tap] = parts[row : row + 8, :32]
                up_out[tap] = parts[64 + row : 64 + row + 8, :32]


def down_weights(w):
    none = jnp.zeros_like(w[:, 0, 0])
    blocks = [w[:, 0, 1], w[:, 0, 2], w[:, 1, 1], w[:, 1, 2], w[:, 2, 1], w[:, 2, 2], none, w[:, 0, 0], w[:, 1, 0], w[:, 2, 0]]
    return jnp.transpose(jnp.stack(blocks, 1), (2, 0, 1, 3)).reshape(32, 240)


def up_weights(w):
    none = jnp.zeros_like(w[0, 0, 0])
    pick = ((1, None), (2, 0))
    rows = []
    for p in range(2):
        for q in range(2):
            for r in range(2):
                row = []
                for k in range(8):
                    a, b, d = pick[p][k // 4], pick[q][k // 2 % 2], pick[r][k % 2]
                    row.append(none if None in (a, b, d) else w[a, b, d])
                rows.append(jnp.concatenate(row, 1))
    return jnp.concatenate(rows, 0)


def exchange(part, axes):
    return lax.all_to_all(part, axes, 0, 0, tiled=True)


def sum_kernel(got, *refs):
    total = jnp.sum(got[...], 0, keepdims=True).astype(refs[-1].dtype)
    refs[-1][...] = jnp.broadcast_to(total, refs[-1].shape)


def sum_spread(got, axes, after=(), dtype=F32):
    return call(sum_kernel, [((lax.axis_size(axes),) + got.shape[1:], dtype)], [got], after=after)[0]


def local(fields, cotangent, w_down, w_mid, w_up):
    w_down_swapped = jnp.swapaxes(w_down, 3, 4)
    wd = down_weights(w_down)
    wg = down_weights(jnp.swapaxes(w_up, 3, 4))
    wm = jnp.transpose(w_mid, (3, 0, 1, 2, 4)).reshape(32, 864)
    wb = jnp.transpose(w_mid[::-1, ::-1, ::-1], (4, 0, 1, 2, 3)).reshape(32, 864)
    none = jnp.zeros((32, 288), BF)
    wb_rows = jnp.stack([jnp.concatenate([wb[:, 576:], none], 1), wb[:, 288:], wb[:, :576], jnp.concatenate([wb[:, :288], none], 1)], 0)
    wu = up_weights(w_up)
    wv = up_weights(w_down_swapped)

    f, g, up, down = call(
        to_slabs_kernel,
        [((4, 8, 16, LANES), BF)] * 2 + [((4, 8, 16, LANES), BF), ((4, 10, 16, LANES), BF)],
        [fields.reshape(256, 256), cotangent.reshape(256, 256)],
    )
    ylo, yhi = shift(up, GY, 1), shift(down, GY, -1)
    f_ext = jnp.concatenate([ylo[:, :5], f, yhi[:, :6]], 1)
    last = jnp.concatenate([f_ext[1:].reshape(57, 16, LANES), ylo[3, 5:], g[3], yhi[3, 6:]], 0)
    xlo = shift(last, GX, 1)
    xhi = shift(f_ext[:2].reshape(38, 16, LANES), GX, -1)

    parts = lax.axis_size(XC)
    grads, slope, h2, d2 = call(
        forward_kernel,
        [((parts, ROWS // parts, LANES), F32), ((15, 32, LANES), F32), ((32, 14 * LANES), BF), ((32, 14 * LANES), BF)],
        [f, g, ylo, yhi, xlo, xhi, wd, wm, wg, wb_rows],
        [((9, 10, 16, LANES), BF), ((5, 8, 16, LANES), BF), ((4, 9, 96, LANES), BF), ((2, 4, 96, LANES), BF),
         ((32, 4 * ROW), F32), ((240, 4 * ROW), BF), ((864, 14 * LANES), BF), ((240, 14 * LANES), BF),
         ((576, 6 * LANES), BF)],
    )

    got = exchange(grads, XC)
    last, first = call(x_rows_kernel, [((7, 32, LANES), BF), ((19, 32, LANES), BF)], [h2, d2], after=[got])
    xlo, xhi = shift(last, GX, 1), shift(first, GX, -1)
    got = exchange(sum_spread(got, Z), Z)
    got = exchange(sum_spread(got, Y), Y)
    mapped, grad_fields = call(
        outputs_kernel,
        [((256, 256), BF)] * 2,
        [f, g, h2, d2, xlo, xhi, slope, wb, wu, wv],
        [((5, 7, 96, LANES), BF), ((864, 15 * LANES), BF), ((32, 15 * LANES), BF), ((256, 8 * LANES), BF), ((512, LANES), BF)],
        flops=10**10,
    )
    grad_down, grad_mid, grad_up = call(
        unpack_kernel,
        [((27, 8, 32), F32), ((27, 32, 32), F32), ((27, 8, 32), F32)],
        [exchange(sum_spread(got, XC, dtype=BF), XC)],
    )
    return (
        mapped.reshape(fields.shape),
        grad_fields.reshape(fields.shape),
        jnp.swapaxes(grad_down.reshape(w_down_swapped.shape), 3, 4),
        grad_mid.reshape(w_mid.shape),
        grad_up.reshape(w_up.shape),
    )


def solution(mesh):
    nx, ny = mesh.devices.shape
    fine = Mesh(mesh.devices.reshape(nx // 4, 4, ny // 4, 2, 2), GX + GY)
    block = P(None, GX, GY, None)
    specs = (block, block, P(), P(), P())
    return jax.shard_map(local, mesh=fine, in_specs=specs, out_specs=specs, check_vma=False)
```

```python
import jax
import jax.numpy as jnp
from jax import lax
from jax.experimental import pallas as pl
from jax.experimental.pallas import tpu as pltpu
from jax.sharding import Mesh
from jax.sharding import PartitionSpec as P

BF = jnp.bfloat16
F32 = jnp.float32
LANES = 128
LOCAL = [(i, j) for i in range(2) for j in range(4)]
UPPER = LOCAL + [(0, 4), (1, 4)] + [(2, j) for j in range(5)]
AROUND = [(i, j) for i in range(-1, 3) for j in range(-1, 5)]
ROW = 6 * LANES
ROWS = 384
GX = ("z", "yl")
GY = ("x", "yh", "core")
XC, Y, Z = ("x", "core"), ("yl", "yh"), ("z",)


def shift(x, axis, by):
    devices = lax.axis_size(axis)
    return lax.ppermute(x, axis, [(i, (i + by) % devices) for i in range(devices)])


def call(body, outs, args, scratch=(), after=(), flops=10**8):
    moved = 2 * 10**6
    return pl.pallas_call(
        body,
        out_shape=[jax.ShapeDtypeStruct(s, d) for s, d in outs],
        in_specs=[pl.BlockSpec(memory_space=pltpu.VMEM)] * len(args) + [pl.BlockSpec(memory_space=pl.ANY)] * len(after),
        out_specs=[pl.BlockSpec(memory_space=pltpu.VMEM)] * len(outs),
        scratch_shapes=[pltpu.VMEM(*s) for s in scratch],
        compiler_params=pltpu.CompilerParams(vmem_limit_bytes=32 * 2**20),
        cost_estimate=pl.CostEstimate(flops=flops, bytes_accessed=moved, transcendentals=0),
    )(*args, *after)


def dot(a, b):
    return lax.dot_general(a, b, (((1,), (0,)), ((), ())), preferred_element_type=F32)


def dot_nt(a, b):
    return lax.dot_general(a, b, (((1,), (1,)), ((), ())), preferred_element_type=F32)


def split_z():
    z = lax.broadcasted_iota(jnp.int32, (256, 256), 0)
    k = lax.broadcasted_iota(jnp.int32, (256, 256), 1)
    return (z == 2 * (k & 127) + (k >> 7)).astype(F32).astype(BF)


def join_z():
    k = lax.broadcasted_iota(jnp.int32, (256, 256), 0)
    z = lax.broadcasted_iota(jnp.int32, (256, 256), 1)
    return (z == 2 * (k & 127) + (k >> 7)).astype(F32).astype(BF)


def slab_order(dim):
    r = lax.broadcasted_iota(jnp.int32, (512, 512), dim)
    s = lax.broadcasted_iota(jnp.int32, (512, 512), 1 - dim)
    source = ((r >> 3) & 1) * 256 + (r & 7) * 32 + (r >> 7) * 8 + ((r >> 4) & 7)
    return (s == source).astype(F32).astype(BF)


def to_slabs_kernel(f_ref, g_ref, f_out, g_out, up_out, down_out):
    halves = split_z()
    order = slab_order(0)
    for ref, out in ((f_ref, f_out), (g_ref, g_out)):
        z = dot(ref[...], halves).astype(BF)
        z = jnp.concatenate([z[:, :LANES], z[:, LANES:]], 0)
        out[...] = dot(order, z).astype(BF).reshape(4, 8, 16, LANES)
    up_out[:, 0:3] = f_out[:, 5:8]
    up_out[:, 3:4] = g_out[:, 7:8]
    down_out[...] = f_out[:, 0:2]


def rolled_odd(slab):
    return pltpu.roll(slab.astype(F32)[8:], 1, 1)


def act_and_slope(v):
    t = jnp.tanh(0.5 * v)
    gain = 0.6 + 0.4 * t
    return v * gain, gain + 0.2 * v * (1.0 - t * t)


def three(v):
    return jnp.concatenate([pltpu.roll(v, 1, 1), v, pltpu.roll(v, LANES - 1, 1)], 0).astype(BF)


def fill_columns(out, n, slab, pair, i, j):
    for a in range(3):
        x = 2 * i + a - 1
        tiles = [slab(x, 2 * j - 1), slab(x, 2 * j), slab(x, 2 * j + 1), pair(x, j - 1), pair(x, j)]
        for t, tile in enumerate(tiles):
            row = 80 * a + 16 * t
            out[row : row + 16, n * LANES : (n + 1) * LANES] = tile


def packed(v, step):
    total = None
    for k in range(4):
        part = v[step * k : step * (k + 1)]
        part = jnp.concatenate([part, jnp.zeros((part.shape[0], 96), F32)], 1)
        if part.shape[0] < step:
            part = jnp.concatenate([part, jnp.zeros((step - part.shape[0], LANES), F32)], 0)
        part = pltpu.roll(part, 32 * k, 1) if k else part
        total = part if total is None else total + part
    return total


def forward_kernel(
    f_ref, g_ref, ylo, yhi, xlo, xhi, wd, wm, wg, wb,
    grads_out, slope_out, h2_out, d2_out,
    fpair, gpair, h1_three, d2_three, slope, xcol, mcol, gcol, zcol,
):
    def f(x, y):
        if x < 0:
            return xlo[(x + 3) * 13 + y + 3]
        if x > 3:
            return xhi[(x - 4) * 13 + y + 3]
        return ylo[x, y + 3] if y < 0 else yhi[x, y - 8] if y > 7 else f_ref[x, y]

    def g(x, y):
        if x < 0:
            return xlo[39 + y + 1]
        return ylo[x, 3] if y < 0 else g_ref[x, y]

    zero = jnp.zeros((8, LANES), F32)
    for x in range(-3, 6):
        for j in range(-2, 5):
            first = zero if j == -2 else rolled_odd(f(x, 2 * j))
            fpair[x + 3, j + 2] = jnp.concatenate([first, rolled_odd(f(x, 2 * j + 1))], 0).astype(BF)
    for x in range(-1, 4):
        for j in range(-1, 4):
            first = zero if j == -1 else rolled_odd(g(x, 2 * j))
            gpair[x + 1, j + 1] = jnp.concatenate([first, rolled_odd(g(x, 2 * j + 1))], 0).astype(BF)

    def f_pair(x, j):
        return fpair[x + 3, j + 2]

    def g_pair(x, j):
        return gpair[x + 1, j + 1]

    for n, (i, j) in enumerate(LOCAL):
        fill_columns(gcol, n, g, g_pair, i, j)
    for n, (i, j) in enumerate(AROUND):
        fill_columns(xcol, n, f, f_pair, i, j)

    for i in range(-1, 3):
        start = (i + 1) * ROW
        v, s = act_and_slope(dot(wd[...], xcol[:, start : start + ROW]))
        slope[:, start : start + ROW] = s
        for j in range(-1, 5):
            lanes = slice((j + 1) * LANES, (j + 2) * LANES)
            h1_three[i + 1, j + 1] = three(v[:, lanes])
            if i >= 0 and j >= 0:
                slope_out[i * 5 + j] = s[:, lanes]

    for n, (i, j) in enumerate(LOCAL):
        for a in range(3):
            for b in range(3):
                row = 96 * (3 * a + b)
                mcol[row : row + 96, n * LANES : (n + 1) * LANES] = h1_three[i + a, j + b]

    for start in range(0, 8, 4):
        lanes = slice(start * LANES, (start + 4) * LANES)
        v, s = act_and_slope(dot(wm[...], mcol[:, lanes]))
        h2_out[:, lanes] = v.astype(BF)
        d2_out[:, lanes] = (dot(wg[...], gcol[:, lanes]) * s).astype(BF)
    for n, (i, j) in enumerate(LOCAL):
        d2_three[i, j] = three(d2_out[:, n * LANES : (n + 1) * LANES].astype(F32))

    down = jnp.zeros((240, 64), F32)
    for i in range(-1, 3):
        inside = [a for a in range(3) if 0 <= i + a - 1 <= 1]
        depth = 288 * len(inside)
        for m, a in enumerate(inside):
            for b in range(3):
                row = 288 * m + 96 * b
                for j in range(-1, 5):
                    lanes = slice((j + 1) * LANES, (j + 2) * LANES)
                    near = 0 <= j + b - 1 <= 3
                    zcol[row : row + 96, lanes] = d2_three[i + a - 1, j + b - 1] if near else jnp.zeros((96, LANES), BF)
        start = (i + 1) * ROW
        part = dot(wb[i + 1, :, :depth], zcol[:depth]) * slope[:, start : start + ROW]
        high = part.astype(BF)
        low = (part - high.astype(F32)).astype(BF)
        down += dot_nt(xcol[:, start : start + ROW], jnp.concatenate([high, low], 0))
    rows = jnp.concatenate(
        [
            packed(dot_nt(mcol[...], d2_out[...]), 224),
            packed(down[:, :32] + down[:, 32:], 64),
            packed(dot_nt(gcol[...], h2_out[...]), 64),
            jnp.zeros((ROWS - 352, LANES), F32),
        ],
        0,
    )
    grads_out[...] = rows.reshape(grads_out.shape)


def y_rows_kernel(h2, d2, after, up_out, down_out):
    for i in range(2):
        at = 4 * i * LANES
        up_out[i] = d2[:, at + 3 * LANES : at + 4 * LANES]
        down_out[i] = d2[:, at : at + LANES]
        down_out[2 + i] = d2[:, at + LANES : at + 2 * LANES]
        down_out[4 + i] = h2[:, at : at + LANES]


def x_rows_kernel(h2, d2, ylo, yhi, up_out, down_out):
    for i in range(2):
        down_out[7 * i] = ylo[i]
        for j in range(4):
            at = (4 * i + j) * LANES
            down_out[7 * i + 1 + j] = d2[:, at : at + LANES]
        down_out[7 * i + 5] = yhi[i]
        down_out[7 * i + 6] = yhi[2 + i]
    for j in range(4):
        down_out[14 + j] = h2[:, j * LANES : (j + 1) * LANES]
    down_out[18] = yhi[4]
    for j in range(7):
        up_out[j] = down_out[7 + j]


def outputs_kernel(
    f_ref, g_ref, h2, d2, ylo, yhi, xlo, xhi, slope, wb, wu, wv,
    mapped_out, grad_out, d2_three, mcol, d1, ucol, slabs,
):
    def d(i, j):
        if i < 0:
            return xlo[j + 1]
        if i > 1:
            return xhi[(i - 2) * 7 + j + 1]
        if j < 0:
            return ylo[i]
        if j > 3:
            return yhi[2 * (j - 4) + i]
        at = (4 * i + j) * LANES
        return d2[:, at : at + LANES]

    for i in range(-1, 4):
        for j in range(-1, 6):
            d2_three[i + 1, j + 1] = three(d(i, j).astype(F32))
    for n, (i, j) in enumerate(UPPER):
        for a in range(3):
            for b in range(3):
                row = 96 * (3 * a + b)
                mcol[row : row + 96, n * LANES : (n + 1) * LANES] = d2_three[i + a, j + b]
    for start in range(0, 15, 4):
        cells = UPPER[start : start + 4]
        v = dot(wb[...], mcol[:, start * LANES : (start + len(cells)) * LANES])
        for n, (i, j) in enumerate(cells):
            at = (start + n) * LANES
            d1[:, at : at + LANES] = (v[:, n * LANES : (n + 1) * LANES] * slope[i * 5 + j]).astype(BF)

    def h(i, j):
        if i > 1:
            return xhi[14 + j]
        if j > 3:
            return yhi[4 + i]
        at = (4 * i + j) * LANES
        return h2[:, at : at + LANES]

    def p(i, j):
        at = UPPER.index((i, j)) * LANES
        return d1[:, at : at + LANES]

    joined = join_z()
    order = slab_order(1)
    for cell, w, base, out in ((h, wu, f_ref, mapped_out), (p, wv, g_ref, grad_out)):
        two = {}
        for i, j in UPPER:
            v = cell(i, j).astype(F32)
            two[i, j] = jnp.concatenate([v, pltpu.roll(v, LANES - 1, 1)], 0).astype(BF)
        for n, (i, j) in enumerate(LOCAL):
            for k in range(4):
                ucol[64 * k : 64 * k + 64, n * LANES : (n + 1) * LANES] = two[i + k // 2, j + k % 2]
        for start in range(0, 8, 2):
            up = dot(w[...], ucol[:, start * LANES : (start + 2) * LANES])
            for n in range(2):
                i, j = LOCAL[start + n]
                for k in range(4):
                    x, y = 2 * i + k // 2, 2 * j + k % 2
                    row = 16 * (8 * x + y)
                    added = base[x, y].astype(F32) + up[16 * k : 16 * k + 16, n * LANES : (n + 1) * LANES]
                    slabs[row : row + 16] = added.astype(BF)
        z = dot(order, slabs[...]).astype(BF)
        out[...] = dot(jnp.concatenate([z[:256], z[256:]], 1), joined).astype(BF)


def tap_rows(rows):
    order = [(0, 1), (0, 2), (1, 1), (1, 2), (2, 1), (2, 2), None, (0, 0), (1, 0), (2, 0)]
    for a in range(3):
        for m, tap in enumerate(order):
            if tap is not None:
                yield 10 * a + m, 9 * a + 3 * tap[0] + tap[1]


def unpack_kernel(total, down_out, mid_out, up_out):
    total = total[...].astype(F32).reshape(ROWS, LANES)
    flipped = jnp.concatenate([total[0:224], jnp.zeros((32, LANES), F32)], 0).T
    for tap in range(27):
        k, m = tap // 7, tap % 7
        rows = flipped[32 * k : 32 * k + 32, LANES * (m // 4) : LANES * (m // 4 + 1)]
        rows = pltpu.roll(rows, LANES - 32 * (m % 4), 1) if m % 4 else rows
        mid_out[tap] = rows[:, :32]
    for k in range(4):
        parts = total[224:352]
        parts = pltpu.roll(parts, LANES - 32 * k, 1) if k else parts
        for block, tap in tap_rows(240):
            if block // 8 == k:
                row = 8 * (block % 8)
                down_out[tap] = parts[row : row + 8, :32]
                up_out[tap] = parts[64 + row : 64 + row + 8, :32]


def down_weights(w):
    none = jnp.zeros_like(w[:, 0, 0])
    blocks = [w[:, 0, 1], w[:, 0, 2], w[:, 1, 1], w[:, 1, 2], w[:, 2, 1], w[:, 2, 2], none, w[:, 0, 0], w[:, 1, 0], w[:, 2, 0]]
    return jnp.transpose(jnp.stack(blocks, 1), (2, 0, 1, 3)).reshape(32, 240)


def up_weights(w):
    none = jnp.zeros_like(w[0, 0, 0])
    pick = ((1, None), (2, 0))
    rows = []
    for p in range(2):
        for q in range(2):
            for r in range(2):
                row = []
                for k in range(8):
                    a, b, d = pick[p][k // 4], pick[q][k // 2 % 2], pick[r][k % 2]
                    row.append(none if None in (a, b, d) else w[a, b, d])
                rows.append(jnp.concatenate(row, 1))
    return jnp.concatenate(rows, 0)


def exchange(part, axes):
    return lax.all_to_all(part, axes, 0, 0, tiled=True)


def sum_kernel(got, out):
    total = jnp.sum(got[...], 0, keepdims=True).astype(out.dtype)
    out[...] = jnp.broadcast_to(total, out.shape)


def sum_spread(got, axes, dtype=F32):
    return call(sum_kernel, [((lax.axis_size(axes),) + got.shape[1:], dtype)], [got])[0]


def local(fields, cotangent, w_down, w_mid, w_up):
    w_down_swapped = jnp.swapaxes(w_down, 3, 4)
    wd = down_weights(w_down)
    wg = down_weights(jnp.swapaxes(w_up, 3, 4))
    wm = jnp.transpose(w_mid, (3, 0, 1, 2, 4)).reshape(32, 864)
    wb = jnp.transpose(w_mid[::-1, ::-1, ::-1], (4, 0, 1, 2, 3)).reshape(32, 864)
    none = jnp.zeros((32, 288), BF)
    wb_rows = jnp.stack([jnp.concatenate([wb[:, 576:], none], 1), wb[:, 288:], wb[:, :576], jnp.concatenate([wb[:, :288], none], 1)], 0)
    wu = up_weights(w_up)
    wv = up_weights(w_down_swapped)

    f, g, up, down = call(
        to_slabs_kernel,
        [((4, 8, 16, LANES), BF)] * 2 + [((4, 4, 16, LANES), BF), ((4, 2, 16, LANES), BF)],
        [fields.reshape(256, 256), cotangent.reshape(256, 256)],
    )
    ylo, yhi = shift(up, GY, 1), shift(down, GY, -1)
    f_ext = jnp.concatenate([ylo[:, :3], f, yhi], 1)
    last = jnp.concatenate([f_ext[1:].reshape(39, 16, LANES), ylo[3, 3:4], g[3]], 0)
    xlo = shift(last, GX, 1)
    xhi = shift(f_ext[:2].reshape(26, 16, LANES), GX, -1)

    parts = lax.axis_size(XC)
    grads, slope, h2, d2 = call(
        forward_kernel,
        [((parts, ROWS // parts, LANES), F32), ((15, 32, LANES), F32), ((32, 8 * LANES), BF), ((32, 8 * LANES), BF)],
        [f, g, ylo, yhi, xlo, xhi, wd, wm, wg, wb_rows],
        [((9, 7, 16, LANES), BF), ((5, 5, 16, LANES), BF), ((4, 6, 96, LANES), BF), ((2, 4, 96, LANES), BF),
         ((32, 4 * ROW), F32), ((240, 4 * ROW), BF), ((864, 8 * LANES), BF), ((240, 8 * LANES), BF), ((576, ROW), BF)],
    )

    got = exchange(grads, XC)
    up, down = call(y_rows_kernel, [((2, 32, LANES), BF), ((6, 32, LANES), BF)], [h2, d2], after=[got])
    ylo, yhi = shift(up, GY, 1), shift(down, GY, -1)
    got = exchange(sum_spread(got, Z), Z)
    last, first = call(
        x_rows_kernel, [((7, 32, LANES), BF), ((19, 32, LANES), BF)], [h2, d2, ylo, yhi], flops=10**10
    )
    xlo, xhi = shift(last, GX, 1), shift(first, GX, -1)
    got = exchange(sum_spread(got, Y), Y)
    mapped, grad_fields = call(
        outputs_kernel,
        [((256, 256), BF)] * 2,
        [f, g, h2, d2, ylo, yhi, xlo, xhi, slope, wb, wu, wv],
        [((5, 7, 96, LANES), BF), ((864, 15 * LANES), BF), ((32, 15 * LANES), BF), ((256, 8 * LANES), BF), ((512, LANES), BF)],
        flops=10**10,
    )
    grad_down, grad_mid, grad_up = call(
        unpack_kernel,
        [((27, 8, 32), F32), ((27, 32, 32), F32), ((27, 8, 32), F32)],
        [exchange(sum_spread(got, XC, dtype=BF), XC)],
    )
    return (
        mapped.reshape(fields.shape),
        grad_fields.reshape(fields.shape),
        jnp.swapaxes(grad_down.reshape(w_down_swapped.shape), 3, 4),
        grad_mid.reshape(w_mid.shape),
        grad_up.reshape(w_up.shape),
    )


def solution(mesh):
    nx, ny = mesh.devices.shape
    fine = Mesh(mesh.devices.reshape(nx // 4, 4, ny // 4, 2, 2), GX + GY)
    block = P(None, GX, GY, None)
    specs = (block, block, P(), P(), P())
    return jax.shard_map(local, mesh=fine, in_specs=specs, out_specs=specs, check_vma=False)
```

```python
import jax
import jax.numpy as jnp
from jax import lax
from jax.experimental import pallas as pl
from jax.experimental.pallas import tpu as pltpu
from jax.sharding import Mesh
from jax.sharding import PartitionSpec as P

BF = jnp.bfloat16
F32 = jnp.float32
LANES = 128
LOCAL = [(i, j) for i in range(2) for j in range(4)]
UPPER = LOCAL + [(0, 4), (1, 4)] + [(2, j) for j in range(5)]
AROUND = [(i, j) for i in range(-1, 3) for j in range(-1, 5)]
ROW = 6 * LANES
ROWS = 384
GX = ("z", "yl")
GY = ("x", "yh", "core")
XC, Y, Z = ("x", "core"), ("yl", "yh"), ("z",)


def shift(x, axis, by):
    devices = lax.axis_size(axis)
    return lax.ppermute(x, axis, [(i, (i + by) % devices) for i in range(devices)])


def call(body, outs, args, scratch=(), after=(), flops=10**8):
    moved = 2 * 10**6
    return pl.pallas_call(
        body,
        out_shape=[jax.ShapeDtypeStruct(s, d) for s, d in outs],
        in_specs=[pl.BlockSpec(memory_space=pltpu.VMEM)] * len(args) + [pl.BlockSpec(memory_space=pl.ANY)] * len(after),
        out_specs=[pl.BlockSpec(memory_space=pltpu.VMEM)] * len(outs),
        scratch_shapes=[pltpu.VMEM(*s) for s in scratch],
        compiler_params=pltpu.CompilerParams(vmem_limit_bytes=32 * 2**20),
        cost_estimate=pl.CostEstimate(flops=flops, bytes_accessed=moved, transcendentals=0),
    )(*args, *after)


def dot(a, b):
    return lax.dot_general(a, b, (((1,), (0,)), ((), ())), preferred_element_type=F32)


def dot_nt(a, b):
    return lax.dot_general(a, b, (((1,), (1,)), ((), ())), preferred_element_type=F32)


def split_z():
    z = lax.broadcasted_iota(jnp.int32, (256, 256), 0)
    k = lax.broadcasted_iota(jnp.int32, (256, 256), 1)
    return (z == 2 * (k & 127) + (k >> 7)).astype(F32).astype(BF)


def join_z():
    k = lax.broadcasted_iota(jnp.int32, (256, 256), 0)
    z = lax.broadcasted_iota(jnp.int32, (256, 256), 1)
    return (z == 2 * (k & 127) + (k >> 7)).astype(F32).astype(BF)


def slab_order(dim):
    r = lax.broadcasted_iota(jnp.int32, (512, 512), dim)
    s = lax.broadcasted_iota(jnp.int32, (512, 512), 1 - dim)
    source = ((r >> 3) & 1) * 256 + (r & 7) * 32 + (r >> 7) * 8 + ((r >> 4) & 7)
    return (s == source).astype(F32).astype(BF)


def to_slabs(ref):
    z = dot(ref[...], split_z()).astype(BF)
    z = jnp.concatenate([z[:, :LANES], z[:, LANES:]], 0)
    return dot(slab_order(0), z).astype(BF).reshape(4, 8, 16, LANES)


def fields_kernel(f_ref, f_out, down_out):
    f_out[...] = to_slabs(f_ref)
    down_out[...] = f_out[:, 0:2]


def cotangent_kernel(g_ref, f_ref, g_out, up_out):
    g_out[...] = to_slabs(g_ref)
    up_out[:, 0:3] = f_ref[:, 5:8]
    up_out[:, 3:4] = g_out[:, 7:8]


def rolled_odd(slab):
    return pltpu.roll(slab.astype(F32)[8:], 1, 1)


def act_and_slope(v):
    t = jnp.tanh(0.5 * v)
    gain = 0.6 + 0.4 * t
    return v * gain, gain + 0.2 * v * (1.0 - t * t)


def three(v):
    return jnp.concatenate([pltpu.roll(v, 1, 1), v, pltpu.roll(v, LANES - 1, 1)], 0).astype(BF)


def fill_columns(out, n, slab, pair, i, j):
    for a in range(3):
        x = 2 * i + a - 1
        tiles = [slab(x, 2 * j - 1), slab(x, 2 * j), slab(x, 2 * j + 1), pair(x, j - 1), pair(x, j)]
        for t, tile in enumerate(tiles):
            row = 80 * a + 16 * t
            out[row : row + 16, n * LANES : (n + 1) * LANES] = tile


def packed(v, step):
    total = None
    for k in range(4):
        part = v[step * k : step * (k + 1)]
        part = jnp.concatenate([part, jnp.zeros((part.shape[0], 96), F32)], 1)
        if part.shape[0] < step:
            part = jnp.concatenate([part, jnp.zeros((step - part.shape[0], LANES), F32)], 0)
        part = pltpu.roll(part, 32 * k, 1) if k else part
        total = part if total is None else total + part
    return total


def forward_kernel(
    f_ref, g_ref, ylo, yhi, xlo, xhi, wd, wm, wg, wb,
    grads_out, slope_out, h2_out, d2_out,
    fpair, gpair, h1_three, d2_three, slope, xcol, mcol, gcol, zcol,
):
    def f(x, y):
        if x < 0:
            return xlo[(x + 3) * 13 + y + 3]
        if x > 3:
            return xhi[(x - 4) * 13 + y + 3]
        return ylo[x, y + 3] if y < 0 else yhi[x, y - 8] if y > 7 else f_ref[x, y]

    def g(x, y):
        if x < 0:
            return xlo[39 + y + 1]
        return ylo[x, 3] if y < 0 else g_ref[x, y]

    zero = jnp.zeros((8, LANES), F32)
    for x in range(-3, 6):
        for j in range(-2, 5):
            first = zero if j == -2 else rolled_odd(f(x, 2 * j))
            fpair[x + 3, j + 2] = jnp.concatenate([first, rolled_odd(f(x, 2 * j + 1))], 0).astype(BF)
    for x in range(-1, 4):
        for j in range(-1, 4):
            first = zero if j == -1 else rolled_odd(g(x, 2 * j))
            gpair[x + 1, j + 1] = jnp.concatenate([first, rolled_odd(g(x, 2 * j + 1))], 0).astype(BF)

    def f_pair(x, j):
        return fpair[x + 3, j + 2]

    def g_pair(x, j):
        return gpair[x + 1, j + 1]

    for n, (i, j) in enumerate(LOCAL):
        fill_columns(gcol, n, g, g_pair, i, j)
    for n, (i, j) in enumerate(AROUND):
        fill_columns(xcol, n, f, f_pair, i, j)

    for i in range(-1, 3):
        start = (i + 1) * ROW
        v, s = act_and_slope(dot(wd[...], xcol[:, start : start + ROW]))
        slope[:, start : start + ROW] = s
        for j in range(-1, 5):
            lanes = slice((j + 1) * LANES, (j + 2) * LANES)
            h1_three[i + 1, j + 1] = three(v[:, lanes])
            if i >= 0 and j >= 0:
                slope_out[i * 5 + j] = s[:, lanes]

    for n, (i, j) in enumerate(LOCAL):
        for a in range(3):
            for b in range(3):
                row = 96 * (3 * a + b)
                mcol[row : row + 96, n * LANES : (n + 1) * LANES] = h1_three[i + a, j + b]

    for start in range(0, 8, 4):
        lanes = slice(start * LANES, (start + 4) * LANES)
        v, s = act_and_slope(dot(wm[...], mcol[:, lanes]))
        h2_out[:, lanes] = v.astype(BF)
        d2_out[:, lanes] = (dot(wg[...], gcol[:, lanes]) * s).astype(BF)
    for n, (i, j) in enumerate(LOCAL):
        d2_three[i, j] = three(d2_out[:, n * LANES : (n + 1) * LANES].astype(F32))

    down = jnp.zeros((240, 64), F32)
    for i in range(-1, 3):
        inside = [a for a in range(3) if 0 <= i + a - 1 <= 1]
        depth = 288 * len(inside)
        for m, a in enumerate(inside):
            for b in range(3):
                row = 288 * m + 96 * b
                for j in range(-1, 5):
                    lanes = slice((j + 1) * LANES, (j + 2) * LANES)
                    near = 0 <= j + b - 1 <= 3
                    zcol[row : row + 96, lanes] = d2_three[i + a - 1, j + b - 1] if near else jnp.zeros((96, LANES), BF)
        start = (i + 1) * ROW
        part = dot(wb[i + 1, :, :depth], zcol[:depth]) * slope[:, start : start + ROW]
        high = part.astype(BF)
        low = (part - high.astype(F32)).astype(BF)
        down += dot_nt(xcol[:, start : start + ROW], jnp.concatenate([high, low], 0))
    rows = jnp.concatenate(
        [
            packed(dot_nt(mcol[...], d2_out[...]), 224),
            packed(down[:, :32] + down[:, 32:], 64),
            packed(dot_nt(gcol[...], h2_out[...]), 64),
            jnp.zeros((ROWS - 352, LANES), F32),
        ],
        0,
    )
    grads_out[...] = rows.reshape(grads_out.shape)


def y_rows_kernel(h2, d2, after, up_out, down_out):
    for i in range(2):
        at = 4 * i * LANES
        up_out[i] = d2[:, at + 3 * LANES : at + 4 * LANES]
        down_out[i] = d2[:, at : at + LANES]
        down_out[2 + i] = d2[:, at + LANES : at + 2 * LANES]
        down_out[4 + i] = h2[:, at : at + LANES]


def x_rows_kernel(h2, d2, ylo, yhi, up_out, down_out):
    for i in range(2):
        down_out[7 * i] = ylo[i]
        for j in range(4):
            at = (4 * i + j) * LANES
            down_out[7 * i + 1 + j] = d2[:, at : at + LANES]
        down_out[7 * i + 5] = yhi[i]
        down_out[7 * i + 6] = yhi[2 + i]
    for j in range(4):
        down_out[14 + j] = h2[:, j * LANES : (j + 1) * LANES]
    down_out[18] = yhi[4]
    for j in range(7):
        up_out[j] = down_out[7 + j]


def outputs_kernel(
    f_ref, g_ref, h2, d2, ylo, yhi, xlo, xhi, slope, wb, wu, wv,
    mapped_out, grad_out, d2_three, mcol, d1, ucol, slabs,
):
    def d(i, j):
        if i < 0:
            return xlo[j + 1]
        if i > 1:
            return xhi[(i - 2) * 7 + j + 1]
        if j < 0:
            return ylo[i]
        if j > 3:
            return yhi[2 * (j - 4) + i]
        at = (4 * i + j) * LANES
        return d2[:, at : at + LANES]

    for i in range(-1, 4):
        for j in range(-1, 6):
            d2_three[i + 1, j + 1] = three(d(i, j).astype(F32))
    for n, (i, j) in enumerate(UPPER):
        for a in range(3):
            for b in range(3):
                row = 96 * (3 * a + b)
                mcol[row : row + 96, n * LANES : (n + 1) * LANES] = d2_three[i + a, j + b]
    for start in range(0, 15, 4):
        cells = UPPER[start : start + 4]
        v = dot(wb[...], mcol[:, start * LANES : (start + len(cells)) * LANES])
        for n, (i, j) in enumerate(cells):
            at = (start + n) * LANES
            d1[:, at : at + LANES] = (v[:, n * LANES : (n + 1) * LANES] * slope[i * 5 + j]).astype(BF)

    def h(i, j):
        if i > 1:
            return xhi[14 + j]
        if j > 3:
            return yhi[4 + i]
        at = (4 * i + j) * LANES
        return h2[:, at : at + LANES]

    def p(i, j):
        at = UPPER.index((i, j)) * LANES
        return d1[:, at : at + LANES]

    joined = join_z()
    order = slab_order(1)
    for cell, w, base, out in ((h, wu, f_ref, mapped_out), (p, wv, g_ref, grad_out)):
        two = {}
        for i, j in UPPER:
            v = cell(i, j).astype(F32)
            two[i, j] = jnp.concatenate([v, pltpu.roll(v, LANES - 1, 1)], 0).astype(BF)
        for n, (i, j) in enumerate(LOCAL):
            for k in range(4):
                ucol[64 * k : 64 * k + 64, n * LANES : (n + 1) * LANES] = two[i + k // 2, j + k % 2]
        for start in range(0, 8, 2):
            up = dot(w[...], ucol[:, start * LANES : (start + 2) * LANES])
            for n in range(2):
                i, j = LOCAL[start + n]
                for k in range(4):
                    x, y = 2 * i + k // 2, 2 * j + k % 2
                    row = 16 * (8 * x + y)
                    added = base[x, y].astype(F32) + up[16 * k : 16 * k + 16, n * LANES : (n + 1) * LANES]
                    slabs[row : row + 16] = added.astype(BF)
        z = dot(order, slabs[...]).astype(BF)
        out[...] = dot(jnp.concatenate([z[:256], z[256:]], 1), joined).astype(BF)


def tap_rows(rows):
    order = [(0, 1), (0, 2), (1, 1), (1, 2), (2, 1), (2, 2), None, (0, 0), (1, 0), (2, 0)]
    for a in range(3):
        for m, tap in enumerate(order):
            if tap is not None:
                yield 10 * a + m, 9 * a + 3 * tap[0] + tap[1]


def unpack_kernel(total, down_out, mid_out, up_out):
    total = total[...].astype(F32).reshape(ROWS, LANES)
    flipped = jnp.concatenate([total[0:224], jnp.zeros((32, LANES), F32)], 0).T
    for tap in range(27):
        k, m = tap // 7, tap % 7
        rows = flipped[32 * k : 32 * k + 32, LANES * (m // 4) : LANES * (m // 4 + 1)]
        rows = pltpu.roll(rows, LANES - 32 * (m % 4), 1) if m % 4 else rows
        mid_out[tap] = rows[:, :32]
    for k in range(4):
        parts = total[224:352]
        parts = pltpu.roll(parts, LANES - 32 * k, 1) if k else parts
        for block, tap in tap_rows(240):
            if block // 8 == k:
                row = 8 * (block % 8)
                down_out[tap] = parts[row : row + 8, :32]
                up_out[tap] = parts[64 + row : 64 + row + 8, :32]


def down_weights(w):
    none = jnp.zeros_like(w[:, 0, 0])
    blocks = [w[:, 0, 1], w[:, 0, 2], w[:, 1, 1], w[:, 1, 2], w[:, 2, 1], w[:, 2, 2], none, w[:, 0, 0], w[:, 1, 0], w[:, 2, 0]]
    return jnp.transpose(jnp.stack(blocks, 1), (2, 0, 1, 3)).reshape(32, 240)


def up_weights(w):
    none = jnp.zeros_like(w[0, 0, 0])
    pick = ((1, None), (2, 0))
    rows = []
    for p in range(2):
        for q in range(2):
            for r in range(2):
                row = []
                for k in range(8):
                    a, b, d = pick[p][k // 4], pick[q][k // 2 % 2], pick[r][k % 2]
                    row.append(none if None in (a, b, d) else w[a, b, d])
                rows.append(jnp.concatenate(row, 1))
    return jnp.concatenate(rows, 0)


def exchange(part, axes):
    return lax.all_to_all(part, axes, 0, 0, tiled=True)


def sum_kernel(got, out):
    total = jnp.sum(got[...], 0, keepdims=True).astype(out.dtype)
    out[...] = jnp.broadcast_to(total, out.shape)


def sum_spread(got, axes, dtype=F32):
    return call(sum_kernel, [((lax.axis_size(axes),) + got.shape[1:], dtype)], [got])[0]


def local(fields, cotangent, w_down, w_mid, w_up):
    w_down_swapped = jnp.swapaxes(w_down, 3, 4)
    wd = down_weights(w_down)
    wg = down_weights(jnp.swapaxes(w_up, 3, 4))
    wm = jnp.transpose(w_mid, (3, 0, 1, 2, 4)).reshape(32, 864)
    wb = jnp.transpose(w_mid[::-1, ::-1, ::-1], (4, 0, 1, 2, 3)).reshape(32, 864)
    none = jnp.zeros((32, 288), BF)
    wb_rows = jnp.stack([jnp.concatenate([wb[:, 576:], none], 1), wb[:, 288:], wb[:, :576], jnp.concatenate([wb[:, :288], none], 1)], 0)
    wu = up_weights(w_up)
    wv = up_weights(w_down_swapped)

    slabs = ((4, 8, 16, LANES), BF)
    f, down = call(fields_kernel, [slabs, ((4, 2, 16, LANES), BF)], [fields.reshape(256, 256)])
    yhi = shift(down, GY, -1)
    g, up = call(cotangent_kernel, [slabs, ((4, 4, 16, LANES), BF)], [cotangent.reshape(256, 256), f], flops=10**10)
    ylo = shift(up, GY, 1)
    f_ext = jnp.concatenate([ylo[:, :3], f, yhi], 1)
    last = jnp.concatenate([f_ext[1:].reshape(39, 16, LANES), ylo[3, 3:4], g[3]], 0)
    xlo = shift(last, GX, 1)
    xhi = shift(f_ext[:2].reshape(26, 16, LANES), GX, -1)

    parts = lax.axis_size(XC)
    grads, slope, h2, d2 = call(
        forward_kernel,
        [((parts, ROWS // parts, LANES), F32), ((15, 32, LANES), F32), ((32, 8 * LANES), BF), ((32, 8 * LANES), BF)],
        [f, g, ylo, yhi, xlo, xhi, wd, wm, wg, wb_rows],
        [((9, 7, 16, LANES), BF), ((5, 5, 16, LANES), BF), ((4, 6, 96, LANES), BF), ((2, 4, 96, LANES), BF),
         ((32, 4 * ROW), F32), ((240, 4 * ROW), BF), ((864, 8 * LANES), BF), ((240, 8 * LANES), BF), ((576, ROW), BF)],
    )

    got = exchange(grads, XC)
    up, down = call(y_rows_kernel, [((2, 32, LANES), BF), ((6, 32, LANES), BF)], [h2, d2], after=[got])
    ylo, yhi = shift(up, GY, 1), shift(down, GY, -1)
    got = exchange(sum_spread(got, Z), Z)
    last, first = call(
        x_rows_kernel, [((7, 32, LANES), BF), ((19, 32, LANES), BF)], [h2, d2, ylo, yhi], flops=10**10
    )
    xlo, xhi = shift(last, GX, 1), shift(first, GX, -1)
    got = exchange(sum_spread(got, Y), Y)
    mapped, grad_fields = call(
        outputs_kernel,
        [((256, 256), BF)] * 2,
        [f, g, h2, d2, ylo, yhi, xlo, xhi, slope, wb, wu, wv],
        [((5, 7, 96, LANES), BF), ((864, 15 * LANES), BF), ((32, 15 * LANES), BF), ((256, 8 * LANES), BF), ((512, LANES), BF)],
        flops=10**10,
    )
    grad_down, grad_mid, grad_up = call(
        unpack_kernel,
        [((27, 8, 32), F32), ((27, 32, 32), F32), ((27, 8, 32), F32)],
        [exchange(sum_spread(got, XC, dtype=BF), XC)],
    )
    return (
        mapped.reshape(fields.shape),
        grad_fields.reshape(fields.shape),
        jnp.swapaxes(grad_down.reshape(w_down_swapped.shape), 3, 4),
        grad_mid.reshape(w_mid.shape),
        grad_up.reshape(w_up.shape),
    )


def solution(mesh):
    nx, ny = mesh.devices.shape
    fine = Mesh(mesh.devices.reshape(nx // 4, 4, ny // 4, 2, 2), GX + GY)
    block = P(None, GX, GY, None)
    specs = (block, block, P(), P(), P())
    return jax.shard_map(local, mesh=fine, in_specs=specs, out_specs=specs, check_vma=False)
```
